32 devices in a mesh: groups: 2 (over y), pool: 4 (over z), head: 4 (over x, core).
Axes of the slice: x: 2, y: 2, z: 4, core: 2. Of those that a mesh axis runs over, the one named last changes fastest.
Arguments:
- hidden: bfloat16 [1280, 8192], P(('groups', 'pool')), parts along dimension 0, may hold values from -96 to 96
- select: int32 [16, 80], P(('groups', 'pool')), parts along dimension 0, may hold values from 0 to 767, as said below
- page_table: int32 [16, 24], P(('groups', 'pool')), parts along dimension 0, may hold values from -1 to 191, as said below
- kv_store: bfloat16 [384, 32, 2048], P(('groups', 'pool'), None, 'head'), parts along dimension 0, may hold values from -6 to 6
- w_query: bfloat16 [8192, 4096], P('pool', 'head'), may hold values from -0.0625 to 0.0625
- w_kv: bfloat16 [8192, 2048], P('pool', 'head'), may hold values from -0.0625 to 0.0625
Outputs:
- attended: bfloat16 [1280, 4096], P(('groups', 'pool'), 'head'), parts along dimension 0
- new_store: bfloat16 [384, 32, 2048], P(('groups', 'pool'), None, 'head'), parts along dimension 0
The draws below stay inside these ranges and needn't reach their ends.
There are 2 independent parts, one for each index of `groups`. The reference program is written for one: setup_inputs(seed, part) draws one part's arguments, and reference() takes and returns one part's arrays. A program takes and returns all parts, laid end to end along the dimension named above; an argument that names none is the same for every part. Nothing has to cross between parts.
Inputs may be any that keep to these rules, and one draw needn't show every extreme that they name: `page_table`: entry (s, p) is the slot holding page p of session s, held by pool device slot // 48, or -1 where the session is shorter; live entries of a session come first, no slot is named twice, and the live entries of the 2 sessions of one pool device name at most 12 slots of any one holder, a count that is reached. `select`: each row holds 80 distinct increasing positions, all on live pages of its session.
All inputs are finite; a program needn't handle non-finite values.
Results may differ from the reference program's by a relative error of at most 0.0045.
The reference program's roundings to bfloat16 on the way (of `queries`, `fresh_rows`, `context` and `weights`) count: a program that leaves them out, or rounds other values in their place, can miss the bound.
Values may be sent and summed in bfloat16 or wider, within the bound.
A program may use at most 128 MiB of HBM per device.

```python
import math
import jax
import jax.numpy as jnp
from jax import lax

D = 8192
HD = 128
KVH = 8
QPK = 4
SESS_DEV = 2
SEL = 80
LEN_MAX = 768
PAGE = 32
PMAX = 24
CAP = 12
SESSIONS = 8
SLOTS = 192
ROWS = 640


def session_lengths(key):
    lower = LEN_MAX // 3
    spread = LEN_MAX - lower
    first_key, second_key = jax.random.split(key)
    draws = jax.random.randint(first_key, (SESSIONS,), 0, spread + 1)
    lengths = lower + draws * draws // spread
    longest = jax.random.randint(second_key, (), 0, SESSIONS)
    return jnp.where(jnp.arange(SESSIONS) == longest, LEN_MAX, lengths).astype(jnp.int32)


def draw_page_table(key, part):
    lengths = session_lengths(key)
    key = jax.random.fold_in(key, 3)
    offset_key, pair_key = jax.random.split(key)
    pool_count = SESSIONS // SESS_DEV
    entry_count = SESS_DEV * PMAX
    offsets = jax.random.permutation(offset_key, pool_count)
    pair_order = jax.vmap(lambda subkey: jax.random.permutation(subkey, entry_count // 2))(jax.random.split(pair_key, pool_count))
    entry_index = jnp.arange(entry_count)
    slot_of = 2 * pair_order[:, entry_index // 2] + entry_index % 2
    owner_index = jnp.arange(pool_count)[:, None]
    holder_of = (owner_index + offsets[slot_of // CAP]) % pool_count
    global_slot = (holder_of * entry_count + slot_of).reshape(SESSIONS, PMAX)
    page_index = jnp.arange(PMAX)[None, :]
    return jnp.where(page_index * PAGE < lengths[:, None], global_slot, -1).astype(jnp.int32)


def draw_select(key, part):
    lengths = session_lengths(key)
    key = jax.random.fold_in(key, 5)
    positions = jnp.arange(LEN_MAX)[None, :]
    scores = jax.random.randint(key, (SESSIONS, LEN_MAX), 0, 2 ** 20) * LEN_MAX + positions
    scores = jnp.where(positions < lengths[:, None], scores, -1)
    chosen = lax.top_k(scores, SEL)[0] % LEN_MAX
    return jnp.sort(chosen, axis=1).astype(jnp.int32)


def draw_hidden(key, part):
    key = jax.random.fold_in(key, 7)
    value_key = jax.random.fold_in(key, 0)
    values = jnp.clip(jax.random.normal(value_key, (ROWS, D), jnp.float32), -6.0, 6.0)
    return values.astype(jnp.bfloat16)


def block_scale(key, extent, cuts, low, high):
    level, own = 1.0, jax.random.fold_in(key, 6)
    for dim, parts in cuts:
        heights = jnp.exp(jax.random.uniform(jax.random.fold_in(own, dim), (parts,), jnp.float32, low / len(cuts), high / len(cuts)))
        level = level * jnp.repeat(heights, extent[dim] // parts).reshape([-1 if axis == dim else 1 for axis in range(len(extent))])
    return level


def normal_values(key, dims, scale, bound, cuts=(), held_as=jnp.bfloat16):
    level = block_scale(key, dims, cuts, -0.22, 0.18) if cuts else 1.0
    values = jax.random.normal(key, dims, jnp.float32) * scale * level
    return jnp.minimum(jnp.maximum(values, -bound), bound).astype(held_as)


def setup_inputs(seed: int = 0, part: int = 0) -> dict:
    seeds = jax.random.split(jax.random.key(seed), 7)
    part_splits = jax.random.split(jax.random.fold_in(seeds[6], part), 7)
    return {
        "hidden": draw_hidden(jax.random.fold_in(jax.random.fold_in(seeds[6], part), 71), part),
        "select": draw_select(jax.random.fold_in(jax.random.fold_in(seeds[6], part), 71), part),
        "page_table": draw_page_table(jax.random.fold_in(jax.random.fold_in(seeds[6], part), 71), part),
        "kv_store": normal_values(part_splits[3], (SLOTS, PAGE, KVH * 2 * HD), 1.0, 6.0, ((0, 4), (2, 4))),
        "w_query": normal_values(seeds[4], (D, KVH * QPK * HD), D ** -0.5, 0.0625, ((0, 4), (1, 4))),
        "w_kv": normal_values(seeds[5], (D, KVH * 2 * HD), D ** -0.5, 0.0625, ((0, 4), (1, 4))),
    }


ROPE_BASE = 500000.0

def rotate_positions(values, positions):
    half_dim = values.shape[-1] // 2
    exponent = jnp.arange(half_dim, dtype=jnp.float32) * 2.0 / values.shape[-1]
    freqs = jnp.power(jnp.float32(ROPE_BASE), -exponent)
    angles = positions.astype(jnp.float32)[:, None] * freqs[None, :]
    cosine = jnp.cos(angles)[:, None, :]
    sine = jnp.sin(angles)[:, None, :]
    first_half = values[..., :half_dim]
    second_half = values[..., half_dim:]
    return jnp.concatenate([first_half * cosine - second_half * sine, second_half * cosine + first_half * sine], axis=-1)

def reference(hidden, select, page_table, kv_store, w_query, w_kv):
    row_count = hidden.shape[0]
    positions = select.reshape(row_count)
    query_sum = jnp.dot(hidden, w_query, preferred_element_type=jnp.float32)
    queries = rotate_positions(query_sum.reshape(row_count, KVH * QPK, HD), positions)
    queries = queries.astype(jnp.bfloat16).reshape(SESSIONS, SEL, KVH, QPK, HD)
    fresh_sum = jnp.dot(hidden, w_kv, preferred_element_type=jnp.float32).reshape(row_count, KVH, 2, HD)
    fresh_keys = rotate_positions(fresh_sum[:, :, 0], positions)
    fresh_rows = jnp.stack([fresh_keys, fresh_sum[:, :, 1]], axis=2).astype(jnp.bfloat16)
    store_width = kv_store.shape[2]
    fresh_rows = fresh_rows.reshape(row_count, store_width)
    page_slots = page_table[jnp.arange(SESSIONS, dtype=jnp.int32)[:, None], select // PAGE]
    flat_index = (page_slots * PAGE + select % PAGE).reshape(row_count).astype(jnp.int32)
    store_rows = kv_store.reshape(SLOTS * PAGE, store_width).at[flat_index].set(fresh_rows)
    new_store = store_rows.reshape(kv_store.shape)

    def attend(inputs):
        table_row, session_queries, session_positions = inputs
        slot_ids = jnp.maximum(table_row, 0)
        row_index = (slot_ids[:, None] * PAGE + jnp.arange(PAGE, dtype=jnp.int32)[None, :]).reshape(LEN_MAX)
        context = store_rows[row_index.astype(jnp.int32)].reshape(LEN_MAX, KVH, 2, HD).astype(jnp.float32)
        cache_keys = context[:, :, 0]
        cache_values = context[:, :, 1]
        scores = jnp.einsum('ikgd,tkd->kgit', session_queries.astype(jnp.float32), cache_keys) / math.sqrt(HD)
        allowed = jnp.arange(LEN_MAX, dtype=jnp.int32)[None, :] <= session_positions[:, None]
        scores = jnp.where(allowed[None, None], scores, -jnp.inf)
        row_peak = lax.optimization_barrier(jnp.max(scores, axis=-1, keepdims=True))
        exps = jnp.exp(scores - row_peak)
        weights = (exps / lax.optimization_barrier(jnp.sum(exps, axis=-1, keepdims=True))).astype(jnp.bfloat16)
        output = jnp.einsum('kgit,tkd->ikgd', weights.astype(jnp.float32), cache_values)
        return output.astype(jnp.bfloat16).reshape(SEL, KVH * QPK * HD)
    attended = lax.map(attend, (page_table, queries, select))
    return (attended.reshape(row_count, KVH * QPK * HD), new_store)
```

```python
import functools
import math

import jax
import jax.numpy as jnp
from jax import lax
from jax.experimental import pallas as pl
from jax.experimental.pallas import tpu as pltpu
from jax.sharding import PartitionSpec as P

HD = 128
ROPE_BASE = 500000.0
MESH = pl.DeviceIdType.MESH
ANY = pl.BlockSpec(memory_space=pl.ANY)
VMEM = pl.BlockSpec(memory_space=pltpu.VMEM)
SMEM = pl.BlockSpec(memory_space=pltpu.SMEM)
LEVELS = 32700.0
VMEM_BYTES = 56 * 1024 * 1024


def holder_rank(table_rows, held_slots):
    is_live = table_rows >= 0
    holder_of = jnp.where(is_live, table_rows // held_slots, -1)
    entry_count = table_rows.shape[0]
    earlier = jnp.arange(entry_count)[None, :] < jnp.arange(entry_count)[:, None]
    same = (holder_of[:, None] == holder_of[None, :]) & earlier & is_live[None, :]
    return is_live, holder_of, jnp.sum(same, axis=1)


def exchange_kernel(
    pool, heads, share, capacity,
    meta, hidden, wq_hbm, wkv_hbm, store_hbm, own_pick, cosine, sine,
    q_out, fresh_all, pages, meta_all,
    wq, wkv, store, own_x, x_in, acc, part_out, scale_out, part_in, scale_in, page_out, fresh,
    picks,
    load_sem, x_send, x_recv, f_send, f_recv, m_send, m_recv, pick_sem,
    g_send, g_recv, p_send, p_recv, s_send, s_recv, r_send, r_recv, own_sem,
):
    me = lax.axis_index("pool")
    head = lax.axis_index("head")
    depth, q_cols = wq.shape
    kv_cols = wkv.shape[1]
    rows = hidden.shape[0]
    piece = depth // share

    def to(offset):
        return lax.rem(me + offset, pool)

    def frm(offset):
        return lax.rem(me + pool - offset, pool)

    loads = [
        pltpu.make_async_copy(store_hbm, store, load_sem.at[0]),
        pltpu.make_async_copy(
            hidden.at[:, pl.ds(pl.multiple_of(me * depth, depth), depth)], own_x, load_sem.at[1]
        ),
        pltpu.make_async_copy(wq_hbm, wq, load_sem.at[2]),
        pltpu.make_async_copy(wkv_hbm, wkv, load_sem.at[3]),
    ]
    for load in loads:
        load.start()

    barrier = pltpu.get_barrier_semaphore()

    @pl.loop(1, pool)
    def _(offset):
        pl.semaphore_signal(barrier, inc=1, device_id={"pool": to(offset)}, device_id_type=MESH)

    for j in range(1, share):
        pl.semaphore_signal(
            barrier, inc=1, device_id={"head": lax.rem(head + j, heads)}, device_id_type=MESH
        )
    pl.semaphore_wait(barrier, pool - 1 + share - 1)

    def meta_copy(offset):
        return pltpu.make_async_remote_copy(
            src_ref=meta.at[to(offset)], dst_ref=meta_all.at[offset],
            send_sem=m_send.at[offset], recv_sem=m_recv.at[offset],
            device_id={"pool": to(offset)}, device_id_type=MESH,
        )

    def x_copy(offset):
        start = to(offset) * depth
        if share > 1:
            start = start + head * piece
        return pltpu.make_async_remote_copy(
            src_ref=hidden.at[:, pl.ds(pl.multiple_of(start, piece), piece)],
            dst_ref=x_in.at[offset, 0],
            send_sem=x_send.at[offset], recv_sem=x_recv.at[offset],
            device_id={"pool": to(offset)}, device_id_type=MESH,
        )

    def share_copy(offset, j):
        return pltpu.make_async_remote_copy(
            src_ref=x_in.at[offset, 0], dst_ref=x_in.at[offset, j],
            send_sem=f_send.at[offset, j], recv_sem=f_recv.at[offset, j],
            device_id={"head": lax.rem(head + j, heads)}, device_id_type=MESH,
        )

    def page_copy(offset):
        return pltpu.make_async_remote_copy(
            src_ref=page_out.at[offset], dst_ref=pages.at[offset],
            send_sem=g_send.at[offset], recv_sem=g_recv.at[offset],
            device_id={"pool": frm(offset)}, device_id_type=MESH,
        )

    def part_copy(offset):
        return pltpu.make_async_remote_copy(
            src_ref=part_out.at[offset], dst_ref=part_in.at[offset],
            send_sem=p_send.at[offset], recv_sem=p_recv.at[offset],
            device_id={"pool": frm(offset)}, device_id_type=MESH,
        )

    def scale_copy(offset):
        return pltpu.make_async_remote_copy(
            src_ref=scale_out.at[offset], dst_ref=scale_in.at[offset],
            send_sem=s_send.at[offset], recv_sem=s_recv.at[offset],
            device_id={"pool": frm(offset)}, device_id_type=MESH,
        )

    def fresh_copy(offset):
        return pltpu.make_async_remote_copy(
            src_ref=fresh, dst_ref=fresh_all.at[offset],
            send_sem=r_send.at[offset], recv_sem=r_recv.at[offset],
            device_id={"pool": to(offset)}, device_id_type=MESH,
        )

    @pl.loop(1, pool)
    def _(offset):
        meta_copy(offset).start()
        x_copy(offset).start()

    own_meta = pltpu.make_async_copy(meta.at[me], meta_all.at[0], own_sem.at[0])
    own_meta.start()
    loads[0].wait()
    for c in range(capacity):
        page_out[0, c] = store[own_pick[0, c]]
    own_pages = pltpu.make_async_copy(page_out.at[0], pages.at[0], own_sem.at[1])
    own_pages.start()

    def pick_copy(offset):
        return pltpu.make_async_copy(
            meta_all.at[offset, :, pl.ds(0, 128)], picks.at[offset], pick_sem.at[offset]
        )

    @pl.loop(1, pool)
    def _(offset):
        meta_copy(offset).wait_recv()
        pick_copy(offset).start()
        pick_copy(offset).wait()
        for c in range(capacity):
            page_out[offset, c] = store[picks[offset, 0, c]]
        page_copy(offset).start()

    for load in loads[1:]:
        load.wait()
    tile = 256 if q_cols % 256 == 0 and kv_cols % 256 == 0 else 128

    def project(x_of, weight, base):
        @pl.loop(0, weight.shape[1] // tile)
        def _(n):
            cols = pl.ds(pl.multiple_of(n * tile, tile), tile)
            total = None
            for x, start in x_of:
                term = jnp.dot(
                    x[...], weight[pl.ds(start, x.shape[1]), cols],
                    preferred_element_type=jnp.float32,
                )
                total = term if total is None else total + term
            acc[:, pl.ds(pl.multiple_of(base + n * tile, tile), tile)] = total

    if share > 1:
        @pl.loop(1, pool)
        def _(offset):
            x_copy(offset).wait_recv()
            for j in range(1, share):
                share_copy(offset, j).start()

    @pl.loop(1, pool)
    def _(offset):
        pieces = []
        if share > 1:
            for j in range(share):
                if j:
                    share_copy(offset, j).wait_recv()
                start = lax.rem(head + heads - j, heads) * piece
                pieces.append((x_in.at[offset, j], pl.multiple_of(start, piece)))
        else:
            x_copy(offset).wait_recv()
            pieces.append((x_in.at[offset, 0], 0))
        project(pieces, wq, 0)
        project(pieces, wkv, q_cols)
        values = acc[...]
        peak = jnp.max(jnp.abs(values), axis=1, keepdims=True)
        scale = jnp.broadcast_to(jnp.maximum(peak * 1.005, 1e-30), (rows, 128)).astype(jnp.bfloat16)
        scale_out[offset] = scale
        inverse = LEVELS / scale.astype(jnp.float32)
        for n in range((q_cols + kv_cols) // 128):
            coded = jnp.round(acc[:, n * 128:(n + 1) * 128] * inverse)
            part_out[offset, :, n * 128:(n + 1) * 128] = coded.astype(jnp.int32).astype(jnp.int16)
        scale_copy(offset).start()
        part_copy(offset).start()

    project([(own_x, 0)], wq, 0)
    project([(own_x, 0)], wkv, q_cols)

    @pl.loop(1, pool)
    def _(offset):
        scale_copy(offset).wait_recv()
        part_copy(offset).wait_recv()
        factor = scale_in[offset].astype(jnp.float32) * (1.0 / LEVELS)
        for n in range((q_cols + kv_cols) // 128):
            cols = slice(n * 128, (n + 1) * 128)
            acc[:, cols] += part_in[offset, :, cols].astype(jnp.int32).astype(jnp.float32) * factor

    def rotated(cols):
        value = acc[:, cols]
        return (value * cosine[...] + pltpu.roll(value, HD // 2, 1) * sine[...]).astype(jnp.bfloat16)

    for n in range(kv_cols // HD):
        cols = slice(q_cols + n * HD, q_cols + (n + 1) * HD)
        block = rotated(cols) if n % 2 == 0 else acc[:, cols].astype(jnp.bfloat16)
        fresh[:, n * HD:(n + 1) * HD] = block

    @pl.loop(1, pool)
    def _(offset):
        fresh_copy(offset).start()

    own_fresh = pltpu.make_async_copy(fresh, fresh_all.at[0], own_sem.at[2])
    own_fresh.start()
    for n in range(q_cols // HD):
        q_out[:, n * HD:(n + 1) * HD] = rotated(slice(n * HD, (n + 1) * HD))

    own_meta.wait()
    own_pages.wait()
    own_fresh.wait()

    @pl.loop(1, pool)
    def _(offset):
        fresh_copy(offset).wait_recv()
        page_copy(offset).wait_recv()
        meta_copy(offset).wait_send()
        x_copy(offset).wait_send()
        for j in range(1, share):
            share_copy(offset, j).wait_send()
        page_copy(offset).wait_send()
        scale_copy(offset).wait_send()
        part_copy(offset).wait_send()
        fresh_copy(offset).wait_send()


def attend_kernel(
    pool, capacity, first_row_unused,
    gather, base, q, fresh_all, pages, meta_all, store, pos_col, pos_row,
    attended, new_store,
    context,
):
    sessions, context_pages = gather.shape
    page_len, width = store.shape[1:]
    context_len = context_pages * page_len
    rows, q_cols = q.shape
    pick = rows // sessions
    local_kv = width // (2 * HD)
    group = q_cols // HD // local_kv
    for s in range(sessions):
        @pl.loop(0, context_pages)
        def _(p):
            context[pl.ds(pl.multiple_of(p * page_len, page_len), page_len), :] = pages[gather[s, p]]

        token = lax.broadcasted_iota(jnp.int32, (context_len, pick), 0)
        hot = jnp.where(token == pos_row[s], 1.0, 0.0).astype(jnp.bfloat16)
        taken = jnp.dot(hot, jnp.ones((pick, HD), jnp.bfloat16), preferred_element_type=jnp.float32) > 0.5
        mine = fresh_all[0, s * pick:(s + 1) * pick, :]
        for n in range(width // HD):
            cols = slice(n * HD, (n + 1) * HD)
            spread = jnp.dot(hot, mine[:, cols], preferred_element_type=jnp.float32)
            context[:, cols] = jnp.where(
                taken, spread, context[:, cols].astype(jnp.float32)
            ).astype(jnp.bfloat16)
        limit = jnp.concatenate([pos_col[s * pick:(s + 1) * pick, :]] * group, axis=0)
        column = lax.broadcasted_iota(jnp.int32, (group * pick, context_len), 1)
        allowed = column <= limit
        for k in range(local_kv):
            keys = context[:, 2 * k * HD:(2 * k + 1) * HD]
            vals = context[:, (2 * k + 1) * HD:(2 * k + 2) * HD]
            heads = jnp.concatenate(
                [
                    q[s * pick:(s + 1) * pick, (k * group + g) * HD:(k * group + g + 1) * HD]
                    for g in range(group)
                ],
                axis=0,
            )
            scores = lax.dot_general(
                heads, keys, (((1,), (1,)), ((), ())), preferred_element_type=jnp.float32
            ) / math.sqrt(HD)
            scores = jnp.where(allowed, scores, -jnp.inf)
            exps = jnp.exp(scores - jnp.max(scores, axis=1, keepdims=True))
            weights = (exps / jnp.sum(exps, axis=1, keepdims=True)).astype(jnp.bfloat16)
            out = jnp.dot(weights, vals, preferred_element_type=jnp.float32).astype(jnp.bfloat16)
            for g in range(group):
                attended[s * pick:(s + 1) * pick, (k * group + g) * HD:(k * group + g + 1) * HD] = (
                    out[g * pick:(g + 1) * pick]
                )

    held = store.shape[0]
    chunk = next(c for c in (8, 6, 4, 3, 2, 1) if held % c == 0)
    span = chunk * page_len

    @pl.loop(0, held // chunk)
    def _(b):
        slots = pl.ds(b * chunk, chunk)
        place = base[0, 0] + b * span + lax.broadcasted_iota(jnp.int32, (span, rows), 0)
        ones = jnp.ones((rows, HD), jnp.bfloat16)

        def add(offset, carry):
            total, count = carry
            goal = meta_all[offset, 1:2, 0:rows]
            hot = jnp.where(place == goal, 1.0, 0.0).astype(jnp.bfloat16)
            total = total + jnp.dot(hot, fresh_all[offset], preferred_element_type=jnp.float32)
            count = count + jnp.dot(hot, ones, preferred_element_type=jnp.float32)
            return total, count

        total, count = lax.fori_loop(
            0, pool, add,
            (jnp.zeros((span, width), jnp.float32), jnp.zeros((span, HD), jnp.float32)),
        )
        taken = count > 0.5
        for n in range(width // HD):
            cols = slice(n * HD, (n + 1) * HD)
            old = store[slots, :, cols].reshape(span, HD).astype(jnp.float32)
            new = jnp.where(taken, total[:, cols], old).astype(jnp.bfloat16)
            new_store[slots, :, cols] = new.reshape(chunk, page_len, HD)


def body(hidden, select, page_table, kv_store, w_query, w_kv):
    rows = hidden.shape[0]
    sessions, pick_count = select.shape
    held_slots, page_len, width = kv_store.shape
    depth, q_cols = w_query.shape
    kv_cols = w_kv.shape[1]
    pool = lax.axis_size("pool")
    heads = lax.axis_size("head")
    me = lax.axis_index("pool")
    share = heads if depth % (128 * heads) == 0 else 1
    context_pages = page_table.shape[1]
    entry_count = sessions * context_pages
    capacity = max(2, 2 * ((entry_count + 2 * pool - 1) // (2 * pool)))
    lanes = 128 * ((max(rows, capacity) + 127) // 128)

    positions = select.reshape(rows)
    half = HD // 2
    freqs = jnp.power(jnp.float32(ROPE_BASE), -(jnp.arange(half, dtype=jnp.float32) * 2.0 / HD))
    angles = positions.astype(jnp.float32)[:, None] * freqs[None, :]
    cosine = jnp.cos(angles)
    sine = jnp.sin(angles)
    cosine = jnp.concatenate([cosine, cosine], axis=1)
    sine = jnp.concatenate([-sine, sine], axis=1)

    table = page_table.reshape(entry_count)
    is_live, holder_of, rank_of = holder_rank(table, held_slots)
    target = jnp.where(is_live, holder_of * capacity + rank_of, -1)
    own_slots = table % held_slots
    request = jnp.max(
        jnp.where(target[:, None] == jnp.arange(pool * capacity)[None, :], own_slots[:, None], 0),
        axis=0,
    ).reshape(pool, capacity).astype(jnp.int32)
    page_of = select // page_len
    slot_of = jnp.max(
        jnp.where(page_of[:, :, None] == jnp.arange(context_pages)[None, None], page_table[:, None, :], -1),
        axis=2,
    )
    goal = (slot_of * page_len + select % page_len).reshape(1, rows)
    meta = jnp.concatenate(
        [
            jnp.pad(request, ((0, 0), (0, lanes - capacity)))[:, None, :],
            jnp.broadcast_to(jnp.pad(goal, ((0, 0), (0, lanes - rows)))[None], (pool, 1, lanes)),
            jnp.zeros((pool, 6, lanes), jnp.int32),
        ],
        axis=1,
    ).astype(jnp.int32)
    own_pick = lax.dynamic_slice_in_dim(request, me, 1, axis=0)
    relative = jnp.where(is_live, (holder_of - me + pool) % pool, 0)
    gather = jnp.where(is_live, relative * capacity + rank_of, 0).reshape(sessions, context_pages)
    gather = gather.astype(jnp.int32)

    bf16, f32, i32 = jnp.bfloat16, jnp.float32, jnp.int32
    cols = q_cols + kv_cols
    dma = pltpu.SemaphoreType.DMA
    q, fresh_all, pages, meta_all = pl.pallas_call(
        functools.partial(exchange_kernel, pool, heads, share, capacity),
        out_shape=(
            jax.ShapeDtypeStruct((rows, q_cols), bf16),
            jax.ShapeDtypeStruct((pool, rows, kv_cols), bf16),
            jax.ShapeDtypeStruct((pool, capacity, page_len, width), bf16),
            jax.ShapeDtypeStruct((pool, 8, lanes), i32),
        ),
        in_specs=[ANY, ANY, ANY, ANY, ANY, SMEM, VMEM, VMEM],
        out_specs=(VMEM, ANY, ANY, ANY),
        scratch_shapes=[
            pltpu.VMEM((depth, q_cols), bf16),
            pltpu.VMEM((depth, kv_cols), bf16),
            pltpu.VMEM((held_slots, page_len, width), bf16),
            pltpu.VMEM((rows, depth), bf16),
            pltpu.VMEM((pool, share, rows, depth // share), bf16),
            pltpu.VMEM((rows, cols), f32),
            pltpu.VMEM((pool, rows, cols), jnp.int16),
            pltpu.VMEM((pool, rows, 128), bf16),
            pltpu.VMEM((pool, rows, cols), jnp.int16),
            pltpu.VMEM((pool, rows, 128), bf16),
            pltpu.VMEM((pool, capacity, page_len, width), bf16),
            pltpu.VMEM((rows, kv_cols), bf16),
            pltpu.SMEM((pool, 8, 128), i32),
            dma((4,)),
            dma((pool,)), dma((pool,)),
            dma((pool, share)), dma((pool, share)),
            dma((pool,)), dma((pool,)), dma((pool,)),
            dma((pool,)), dma((pool,)),
            dma((pool,)), dma((pool,)),
            dma((pool,)), dma((pool,)),
            dma((pool,)), dma((pool,)),
            dma((3,)),
        ],
        compiler_params=pltpu.CompilerParams(
            collective_id=0, has_side_effects=True, vmem_limit_bytes=VMEM_BYTES
        ),
    )(meta, hidden, w_query, w_kv, kv_store, own_pick, cosine, sine)

    base = (me * held_slots * page_len).astype(i32).reshape(1, 1)
    attended, new_store = pl.pallas_call(
        functools.partial(attend_kernel, pool, capacity, 0),
        out_shape=(
            jax.ShapeDtypeStruct((rows, q_cols), bf16),
            jax.ShapeDtypeStruct(kv_store.shape, bf16),
        ),
        in_specs=[SMEM, SMEM] + [VMEM] * 7,
        out_specs=(VMEM, VMEM),
        scratch_shapes=[pltpu.VMEM((context_pages * page_len, width), bf16)],
        compiler_params=pltpu.CompilerParams(vmem_limit_bytes=VMEM_BYTES),
    )(
        gather, base, q, fresh_all,
        pages.reshape(pool * capacity, page_len, width), meta_all, kv_store,
        select.reshape(rows, 1), select.reshape(sessions, 1, pick_count),
    )
    return attended, new_store


def solution(mesh):
    return jax.shard_map(
        body,
        mesh=mesh,
        in_specs=(
            P(("groups", "pool"), None),
            P(("groups", "pool"), None),
            P(("groups", "pool"), None),
            P(("groups", "pool"), None, "head"),
            P("pool", "head"),
            P("pool", "head"),
        ),
        out_specs=(P(("groups", "pool"), "head"), P(("groups", "pool"), None, "head")),
        check_vma=False,
    )
```

```python
import functools
import math

import jax
import jax.numpy as jnp
from jax import lax
from jax.experimental import pallas as pl
from jax.experimental.pallas import tpu as pltpu
from jax.sharding import PartitionSpec as P

HD = 128
ROPE_BASE = 500000.0
MESH = pl.DeviceIdType.MESH
ANY = pl.BlockSpec(memory_space=pl.ANY)
VMEM = pl.BlockSpec(memory_space=pltpu.VMEM)
SMEM = pl.BlockSpec(memory_space=pltpu.SMEM)
LEVELS = 519000.0
VMEM_BYTES = 56 * 1024 * 1024


def holder_rank(table_rows, held_slots):
    is_live = table_rows >= 0
    holder_of = jnp.where(is_live, table_rows // held_slots, -1)
    entry_count = table_rows.shape[0]
    earlier = jnp.arange(entry_count)[None, :] < jnp.arange(entry_count)[:, None]
    same = (holder_of[:, None] == holder_of[None, :]) & earlier & is_live[None, :]
    return is_live, holder_of, jnp.sum(same, axis=1)


def exchange_kernel(
    pool, heads, share, capacity,
    meta, hidden, wq_hbm, wkv_hbm, store_hbm, own_pick, cosine, sine,
    q_out, fresh_all, pages, meta_all,
    wq, wkv, store, own_x, x_in, acc, kv_out, kv_scale, kv_in, kv_scale_in, q_part, q_scale, q_in, q_scale_in,
    page_out, fresh,
    picks,
    load_sem, x_send, x_recv, f_send, f_recv, m_send, m_recv, pick_sem,
    g_send, g_recv, kv_send, kv_recv, q_send, q_recv, r_send, r_recv, own_sem,
):
    me = lax.axis_index("pool")
    head = lax.axis_index("head")
    depth, q_cols = wq.shape
    kv_cols = wkv.shape[1]
    rows = hidden.shape[0]
    piece = depth // share

    def to(offset):
        return lax.rem(me + offset, pool)

    def frm(offset):
        return lax.rem(me + pool - offset, pool)

    loads = [
        pltpu.make_async_copy(store_hbm, store, load_sem.at[0]),
        pltpu.make_async_copy(
            hidden.at[:, pl.ds(pl.multiple_of(me * depth, depth), depth)], own_x, load_sem.at[1]
        ),
        pltpu.make_async_copy(wq_hbm, wq, load_sem.at[2]),
        pltpu.make_async_copy(wkv_hbm, wkv, load_sem.at[3]),
    ]
    for load in loads:
        load.start()

    barrier = pltpu.get_barrier_semaphore()

    @pl.loop(1, pool)
    def _(offset):
        pl.semaphore_signal(barrier, inc=1, device_id={"pool": to(offset)}, device_id_type=MESH)

    for j in range(1, share):
        pl.semaphore_signal(
            barrier, inc=1, device_id={"head": lax.rem(head + j, heads)}, device_id_type=MESH
        )
    pl.semaphore_wait(barrier, pool - 1 + share - 1)

    def meta_copy(offset):
        return pltpu.make_async_remote_copy(
            src_ref=meta.at[to(offset)], dst_ref=meta_all.at[offset],
            send_sem=m_send.at[offset], recv_sem=m_recv.at[offset],
            device_id={"pool": to(offset)}, device_id_type=MESH,
        )

    def x_copy(offset):
        start = to(offset) * depth
        if share > 1:
            start = start + head * piece
        return pltpu.make_async_remote_copy(
            src_ref=hidden.at[:, pl.ds(pl.multiple_of(start, piece), piece)],
            dst_ref=x_in.at[offset, 0],
            send_sem=x_send.at[offset], recv_sem=x_recv.at[offset],
            device_id={"pool": to(offset)}, device_id_type=MESH,
        )

    def share_copy(offset, j):
        return pltpu.make_async_remote_copy(
            src_ref=x_in.at[offset, 0], dst_ref=x_in.at[offset, j],
            send_sem=f_send.at[offset, j], recv_sem=f_recv.at[offset, j],
            device_id={"head": lax.rem(head + j, heads)}, device_id_type=MESH,
        )

    def page_copy(offset):
        return pltpu.make_async_remote_copy(
            src_ref=page_out.at[offset], dst_ref=pages.at[offset],
            send_sem=g_send.at[offset], recv_sem=g_recv.at[offset],
            device_id={"pool": frm(offset)}, device_id_type=MESH,
        )

    def line_copy(bufs, t, going_right):
        out, scale, inbound, scale_in, send, recv = bufs
        side = 0 if going_right else 1
        peer = me + 1 if going_right else me - 1
        return [
            pltpu.make_async_remote_copy(
                src_ref=source.at[t], dst_ref=target.at[side, t],
                send_sem=send.at[k, t], recv_sem=recv.at[side, k, t],
                device_id={"pool": peer}, device_id_type=MESH,
            )
            for k, (source, target) in enumerate(((scale, scale_in), (out, inbound)))
        ]

    def fresh_copy(offset):
        return pltpu.make_async_remote_copy(
            src_ref=fresh, dst_ref=fresh_all.at[offset],
            send_sem=r_send.at[offset], recv_sem=r_recv.at[offset],
            device_id={"pool": to(offset)}, device_id_type=MESH,
        )

    def far_first(send, toward):
        @pl.loop(0, pool - 1)
        def _(step):
            distance = pool - 1 - step

            @pl.when(me + distance < pool)
            def _():
                send(distance if toward else pool - distance)

            @pl.when(me - distance >= 0)
            def _():
                send(pool - distance if toward else distance)

    def send_hidden(offset):
        meta_copy(offset).start()
        x_copy(offset).start()

    far_first(send_hidden, True)

    own_meta = pltpu.make_async_copy(meta.at[me], meta_all.at[0], own_sem.at[0])
    own_meta.start()
    loads[0].wait()
    for c in range(capacity):
        page_out[0, c] = store[own_pick[0, c]]
    own_pages = pltpu.make_async_copy(page_out.at[0], pages.at[0], own_sem.at[1])
    own_pages.start()

    def pick_copy(offset):
        return pltpu.make_async_copy(
            meta_all.at[offset, :, pl.ds(0, 128)], picks.at[offset], pick_sem.at[offset]
        )

    @pl.loop(1, pool)
    def _(offset):
        meta_copy(offset).wait_recv()
        pick_copy(offset).start()
        pick_copy(offset).wait()
        for c in range(capacity):
            page_out[offset, c] = store[picks[offset, 0, c]]
        page_copy(offset).start()

    for load in loads[1:]:
        load.wait()
    tile = 256 if q_cols % 256 == 0 and kv_cols % 256 == 0 else 128

    def project(x_of, weight, base):
        @pl.loop(0, weight.shape[1] // tile)
        def _(n):
            cols = pl.ds(pl.multiple_of(n * tile, tile), tile)
            total = None
            for x, start in x_of:
                term = jnp.dot(
                    x[...], weight[pl.ds(start, x.shape[1]), cols],
                    preferred_element_type=jnp.float32,
                )
                total = term if total is None else total + term
            acc[:, pl.ds(pl.multiple_of(base + n * tile, tile), tile)] = total

    if share > 1:
        def pass_on(offset):
            x_copy(offset).wait_recv()
            for j in range(1, share):
                share_copy(offset, j).start()

        far_first(pass_on, False)

    def encode(bufs, t, base, blocks):
        values = acc[:, base:base + blocks * 128]
        peak = jnp.max(jnp.abs(values), axis=1, keepdims=True)
        scale = jnp.broadcast_to(jnp.maximum(peak * 1.005, 1e-30), (rows, 128)).astype(jnp.bfloat16)
        bufs[1][t] = scale
        inverse = LEVELS / scale.astype(jnp.float32)
        for quad in range(0, blocks, 4):
            packed = jnp.full((rows, 128), -32768, jnp.int32)
            for n in range(quad, min(quad + 4, blocks)):
                code = jnp.round(acc[:, base + n * 128:base + (n + 1) * 128] * inverse).astype(jnp.int32)
                bufs[0][t, :, n * 128:(n + 1) * 128] = (code >> 4).astype(jnp.int16)
                packed = packed + ((code & 15) << (4 * (n - quad)))
            lane = (blocks + quad // 4) * 128
            bufs[0][t, :, lane:lane + 128] = packed.astype(jnp.int16)

    def add_in(bufs, t, side, base, blocks):
        for copy in line_copy(bufs, t, side == 0):
            copy.wait_recv()
        factor = bufs[3][side, t].astype(jnp.float32) * (1.0 / LEVELS)
        for quad in range(0, blocks, 4):
            lane = (blocks + quad // 4) * 128
            packed = bufs[2][side, t, :, lane:lane + 128].astype(jnp.int32) + 32768
            for n in range(quad, min(quad + 4, blocks)):
                high = bufs[2][side, t, :, n * 128:(n + 1) * 128].astype(jnp.int32)
                code = high * 16 + ((packed >> (4 * (n - quad))) & 15)
                acc[:, base + n * 128:base + (n + 1) * 128] += code.astype(jnp.float32) * factor

    def reduce_line(bufs, weight, base, first):
        blocks = weight.shape[1] // 128

        def serve(t, going_right):
            slot = lax.rem(me - t + pool, pool)
            pieces = []
            for j in range(share):
                if first:
                    if j:
                        share_copy(slot, j).wait_recv()
                    elif share == 1:
                        x_copy(slot).wait_recv()
                start = pl.multiple_of(lax.rem(head + heads - j, heads) * piece, piece) if share > 1 else 0
                pieces.append((x_in.at[slot, j], start))
            project(pieces, weight, base)
            side = 0 if going_right else 1

            @pl.when(me > 0 if going_right else me < pool - 1)
            def _():
                add_in(bufs, t, side, base, blocks)

            encode(bufs, t, base, blocks)
            for copy in line_copy(bufs, t, going_right):
                copy.start()

        @pl.loop(0, pool - 1)
        def _(step):
            distance = pool - 1 - step

            @pl.when(me + distance < pool)
            def _():
                serve(me + distance, True)

            @pl.when(me - distance >= 0)
            def _():
                serve(me - distance, False)

        project([(own_x, 0)], weight, base)

        @pl.when(me > 0)
        def _():
            add_in(bufs, me, 0, base, blocks)

        @pl.when(me < pool - 1)
        def _():
            add_in(bufs, me, 1, base, blocks)

    def finish_line(bufs):
        @pl.loop(0, pool)
        def _(t):
            @pl.when(t > me)
            def _():
                for copy in line_copy(bufs, t, True):
                    copy.wait_send()

            @pl.when(t < me)
            def _():
                for copy in line_copy(bufs, t, False):
                    copy.wait_send()

    kv_bufs = (kv_out, kv_scale, kv_in, kv_scale_in, kv_send, kv_recv)
    q_bufs = (q_part, q_scale, q_in, q_scale_in, q_send, q_recv)
    reduce_line(kv_bufs, wkv, q_cols, True)

    def rotated(cols):
        value = acc[:, cols]
        return (value * cosine[...] + pltpu.roll(value, HD // 2, 1) * sine[...]).astype(jnp.bfloat16)

    for n in range(kv_cols // HD):
        cols = slice(q_cols + n * HD, q_cols + (n + 1) * HD)
        block = rotated(cols) if n % 2 == 0 else acc[:, cols].astype(jnp.bfloat16)
        fresh[:, n * HD:(n + 1) * HD] = block

    @pl.loop(1, pool)
    def _(offset):
        fresh_copy(offset).start()

    own_fresh = pltpu.make_async_copy(fresh, fresh_all.at[0], own_sem.at[2])
    own_fresh.start()
    reduce_line(q_bufs, wq, 0, False)
    for n in range(q_cols // HD):
        q_out[:, n * HD:(n + 1) * HD] = rotated(slice(n * HD, (n + 1) * HD))

    own_meta.wait()
    own_pages.wait()
    own_fresh.wait()

    @pl.loop(1, pool)
    def _(offset):
        fresh_copy(offset).wait_recv()
        page_copy(offset).wait_recv()
        meta_copy(offset).wait_send()
        x_copy(offset).wait_send()
        for j in range(1, share):
            share_copy(offset, j).wait_send()
        page_copy(offset).wait_send()
        fresh_copy(offset).wait_send()

    finish_line(kv_bufs)
    finish_line(q_bufs)


def attend_kernel(
    pool, capacity, first_row_unused,
    gather, base, q, fresh_all, pages, meta_all, store, pos_col, pos_row,
    attended, new_store,
    context,
):
    sessions, context_pages = gather.shape
    page_len, width = store.shape[1:]
    context_len = context_pages * page_len
    rows, q_cols = q.shape
    pick = rows // sessions
    local_kv = width // (2 * HD)
    group = q_cols // HD // local_kv
    for s in range(sessions):
        @pl.loop(0, context_pages)
        def _(p):
            context[pl.ds(pl.multiple_of(p * page_len, page_len), page_len), :] = pages[gather[s, p]]

        token = lax.broadcasted_iota(jnp.int32, (context_len, pick), 0)
        hot = jnp.where(token == pos_row[s], 1.0, 0.0).astype(jnp.bfloat16)
        taken = jnp.dot(hot, jnp.ones((pick, HD), jnp.bfloat16), preferred_element_type=jnp.float32) > 0.5
        mine = fresh_all[0, s * pick:(s + 1) * pick, :]
        for n in range(width // HD):
            cols = slice(n * HD, (n + 1) * HD)
            spread = jnp.dot(hot, mine[:, cols], preferred_element_type=jnp.float32)
            context[:, cols] = jnp.where(
                taken, spread, context[:, cols].astype(jnp.float32)
            ).astype(jnp.bfloat16)
        limit = jnp.concatenate([pos_col[s * pick:(s + 1) * pick, :]] * group, axis=0)
        column = lax.broadcasted_iota(jnp.int32, (group * pick, context_len), 1)
        allowed = column <= limit
        for k in range(local_kv):
            keys = context[:, 2 * k * HD:(2 * k + 1) * HD]
            vals = context[:, (2 * k + 1) * HD:(2 * k + 2) * HD]
            heads = jnp.concatenate(
                [
                    q[s * pick:(s + 1) * pick, (k * group + g) * HD:(k * group + g + 1) * HD]
                    for g in range(group)
                ],
                axis=0,
            )
            scores = lax.dot_general(
                heads, keys, (((1,), (1,)), ((), ())), preferred_element_type=jnp.float32
            ) / math.sqrt(HD)
            scores = jnp.where(allowed, scores, -jnp.inf)
            exps = jnp.exp(scores - jnp.max(scores, axis=1, keepdims=True))
            weights = (exps / jnp.sum(exps, axis=1, keepdims=True)).astype(jnp.bfloat16)
            out = jnp.dot(weights, vals, preferred_element_type=jnp.float32).astype(jnp.bfloat16)
            for g in range(group):
                attended[s * pick:(s + 1) * pick, (k * group + g) * HD:(k * group + g + 1) * HD] = (
                    out[g * pick:(g + 1) * pick]
                )

    held = store.shape[0]
    chunk = next(c for c in (8, 6, 4, 3, 2, 1) if held % c == 0)
    span = chunk * page_len

    @pl.loop(0, held // chunk)
    def _(b):
        slots = pl.ds(b * chunk, chunk)
        place = base[0, 0] + b * span + lax.broadcasted_iota(jnp.int32, (span, rows), 0)
        ones = jnp.ones((rows, HD), jnp.bfloat16)

        def add(offset, carry):
            total, count = carry
            goal = meta_all[offset, 1:2, 0:rows]
            hot = jnp.where(place == goal, 1.0, 0.0).astype(jnp.bfloat16)
            total = total + jnp.dot(hot, fresh_all[offset], preferred_element_type=jnp.float32)
            count = count + jnp.dot(hot, ones, preferred_element_type=jnp.float32)
            return total, count

        total, count = lax.fori_loop(
            0, pool, add,
            (jnp.zeros((span, width), jnp.float32), jnp.zeros((span, HD), jnp.float32)),
        )
        taken = count > 0.5
        for n in range(width // HD):
            cols = slice(n * HD, (n + 1) * HD)
            old = store[slots, :, cols].reshape(span, HD).astype(jnp.float32)
            new = jnp.where(taken, total[:, cols], old).astype(jnp.bfloat16)
            new_store[slots, :, cols] = new.reshape(chunk, page_len, HD)


def body(hidden, select, page_table, kv_store, w_query, w_kv):
    rows = hidden.shape[0]
    sessions, pick_count = select.shape
    held_slots, page_len, width = kv_store.shape
    depth, q_cols = w_query.shape
    kv_cols = w_kv.shape[1]
    pool = lax.axis_size("pool")
    heads = lax.axis_size("head")
    me = lax.axis_index("pool")
    share = heads if depth % (128 * heads) == 0 else 1
    context_pages = page_table.shape[1]
    entry_count = sessions * context_pages
    capacity = max(2, 2 * ((entry_count + 2 * pool - 1) // (2 * pool)))
    lanes = 128 * ((max(rows, capacity) + 127) // 128)

    positions = select.reshape(rows)
    half = HD // 2
    freqs = jnp.power(jnp.float32(ROPE_BASE), -(jnp.arange(half, dtype=jnp.float32) * 2.0 / HD))
    angles = positions.astype(jnp.float32)[:, None] * freqs[None, :]
    cosine = jnp.cos(angles)
    sine = jnp.sin(angles)
    cosine = jnp.concatenate([cosine, cosine], axis=1)
    sine = jnp.concatenate([-sine, sine], axis=1)

    table = page_table.reshape(entry_count)
    is_live, holder_of, rank_of = holder_rank(table, held_slots)
    target = jnp.where(is_live, holder_of * capacity + rank_of, -1)
    own_slots = table % held_slots
    request = jnp.max(
        jnp.where(target[:, None] == jnp.arange(pool * capacity)[None, :], own_slots[:, None], 0),
        axis=0,
    ).reshape(pool, capacity).astype(jnp.int32)
    page_of = select // page_len
    slot_of = jnp.max(
        jnp.where(page_of[:, :, None] == jnp.arange(context_pages)[None, None], page_table[:, None, :], -1),
        axis=2,
    )
    goal = (slot_of * page_len + select % page_len).reshape(1, rows)
    meta = jnp.concatenate(
        [
            jnp.pad(request, ((0, 0), (0, lanes - capacity)))[:, None, :],
            jnp.broadcast_to(jnp.pad(goal, ((0, 0), (0, lanes - rows)))[None], (pool, 1, lanes)),
            jnp.zeros((pool, 6, lanes), jnp.int32),
        ],
        axis=1,
    ).astype(jnp.int32)
    own_pick = lax.dynamic_slice_in_dim(request, me, 1, axis=0)
    relative = jnp.where(is_live, (holder_of - me + pool) % pool, 0)
    gather = jnp.where(is_live, relative * capacity + rank_of, 0).reshape(sessions, context_pages)
    gather = gather.astype(jnp.int32)

    bf16, f32, i32 = jnp.bfloat16, jnp.float32, jnp.int32
    cols = q_cols + kv_cols
    dma = pltpu.SemaphoreType.DMA

    def line_scratch(width):
        coded = width + 128 * ((width // 128 + 3) // 4)
        return (
            pltpu.VMEM((pool, rows, coded), jnp.int16),
            pltpu.VMEM((pool, rows, 128), bf16),
            pltpu.VMEM((2, pool, rows, coded), jnp.int16),
            pltpu.VMEM((2, pool, rows, 128), bf16),
        )

    q, fresh_all, pages, meta_all = pl.pallas_call(
        functools.partial(exchange_kernel, pool, heads, share, capacity),
        out_shape=(
            jax.ShapeDtypeStruct((rows, q_cols), bf16),
            jax.ShapeDtypeStruct((pool, rows, kv_cols), bf16),
            jax.ShapeDtypeStruct((pool, capacity, page_len, width), bf16),
            jax.ShapeDtypeStruct((pool, 8, lanes), i32),
        ),
        in_specs=[ANY, ANY, ANY, ANY, ANY, SMEM, VMEM, VMEM],
        out_specs=(VMEM, ANY, ANY, ANY),
        scratch_shapes=[
            pltpu.VMEM((depth, q_cols), bf16),
            pltpu.VMEM((depth, kv_cols), bf16),
            pltpu.VMEM((held_slots, page_len, width), bf16),
            pltpu.VMEM((rows, depth), bf16),
            pltpu.VMEM((pool, share, rows, depth // share), bf16),
            pltpu.VMEM((rows, cols), f32),
            *line_scratch(kv_cols),
            *line_scratch(q_cols),
            pltpu.VMEM((pool, capacity, page_len, width), bf16),
            pltpu.VMEM((rows, kv_cols), bf16),
            pltpu.SMEM((pool, 8, 128), i32),
            dma((4,)),
            dma((pool,)), dma((pool,)),
            dma((pool, share)), dma((pool, share)),
            dma((pool,)), dma((pool,)), dma((pool,)),
            dma((pool,)), dma((pool,)),
            dma((2, pool)), dma((2, 2, pool)),
            dma((2, pool)), dma((2, 2, pool)),
            dma((pool,)), dma((pool,)),
            dma((3,)),
        ],
        compiler_params=pltpu.CompilerParams(
            collective_id=0, has_side_effects=True, vmem_limit_bytes=VMEM_BYTES
        ),
    )(meta, hidden, w_query, w_kv, kv_store, own_pick, cosine, sine)

    base = (me * held_slots * page_len).astype(i32).reshape(1, 1)
    attended, new_store = pl.pallas_call(
        functools.partial(attend_kernel, pool, capacity, 0),
        out_shape=(
            jax.ShapeDtypeStruct((rows, q_cols), bf16),
            jax.ShapeDtypeStruct(kv_store.shape, bf16),
        ),
        in_specs=[SMEM, SMEM] + [VMEM] * 7,
        out_specs=(VMEM, VMEM),
        scratch_shapes=[pltpu.VMEM((context_pages * page_len, width), bf16)],
        compiler_params=pltpu.CompilerParams(vmem_limit_bytes=VMEM_BYTES),
    )(
        gather, base, q, fresh_all,
        pages.reshape(pool * capacity, page_len, width), meta_all, kv_store,
        select.reshape(rows, 1), select.reshape(sessions, 1, pick_count),
    )
    return attended, new_store


def solution(mesh):
    return jax.shard_map(
        body,
        mesh=mesh,
        in_specs=(
            P(("groups", "pool"), None),
            P(("groups", "pool"), None),
            P(("groups", "pool"), None),
            P(("groups", "pool"), None, "head"),
            P("pool", "head"),
            P("pool", "head"),
        ),
        out_specs=(P(("groups", "pool"), "head"), P(("groups", "pool"), None, "head")),
        check_vma=False,
    )
```

```python
import functools
import math

import jax
import jax.numpy as jnp
from jax import lax
from jax.experimental import pallas as pl
from jax.experimental.pallas import tpu as pltpu
from jax.sharding import PartitionSpec as P

HD = 128
ROPE_BASE = 500000.0
MESH = pl.DeviceIdType.MESH
ANY = pl.BlockSpec(memory_space=pl.ANY)
VMEM = pl.BlockSpec(memory_space=pltpu.VMEM)
SMEM = pl.BlockSpec(memory_space=pltpu.SMEM)
LEVELS = 519000.0
VMEM_BYTES = 56 * 1024 * 1024


def holder_rank(table_rows, held_slots):
    is_live = table_rows >= 0
    holder_of = jnp.where(is_live, table_rows // held_slots, -1)
    entry_count = table_rows.shape[0]
    earlier = jnp.arange(entry_count)[None, :] < jnp.arange(entry_count)[:, None]
    same = (holder_of[:, None] == holder_of[None, :]) & earlier & is_live[None, :]
    return is_live, holder_of, jnp.sum(same, axis=1)


def exchange_kernel(
    pool, heads, share, capacity,
    meta, hidden, wq_hbm, wkv_hbm, store_hbm, own_pick, cosine, sine,
    q_out, fresh_all, pages, meta_all,
    wq, wkv, store, own_x, x_in, acc, own_acc, kv_out, kv_scale, kv_in, kv_scale_in, q_part, q_scale, q_in, q_scale_in,
    page_out, fresh,
    picks,
    load_sem, x_send, x_recv, f_send, f_recv, m_send, m_recv, pick_sem,
    g_send, g_recv, kv_send, kv_recv, q_send, q_recv, r_send, r_recv, own_sem,
):
    me = lax.axis_index("pool")
    head = lax.axis_index("head")
    depth, q_cols = wq.shape
    kv_cols = wkv.shape[1]
    rows = hidden.shape[0]
    piece = depth // share

    def to(offset):
        return lax.rem(me + offset, pool)

    def frm(offset):
        return lax.rem(me + pool - offset, pool)

    loads = [
        pltpu.make_async_copy(store_hbm, store, load_sem.at[0]),
        pltpu.make_async_copy(
            hidden.at[:, pl.ds(pl.multiple_of(me * depth, depth), depth)], own_x, load_sem.at[1]
        ),
        pltpu.make_async_copy(wq_hbm, wq, load_sem.at[2]),
        pltpu.make_async_copy(wkv_hbm, wkv, load_sem.at[3]),
    ]
    for load in loads:
        load.start()

    barrier = pltpu.get_barrier_semaphore()

    @pl.loop(1, pool)
    def _(offset):
        pl.semaphore_signal(barrier, inc=1, device_id={"pool": to(offset)}, device_id_type=MESH)

    for j in range(1, share):
        pl.semaphore_signal(
            barrier, inc=1, device_id={"head": lax.rem(head + j, heads)}, device_id_type=MESH
        )
    pl.semaphore_wait(barrier, pool - 1 + share - 1)

    def meta_copy(offset):
        return pltpu.make_async_remote_copy(
            src_ref=meta.at[to(offset)], dst_ref=meta_all.at[offset],
            send_sem=m_send.at[offset], recv_sem=m_recv.at[offset],
            device_id={"pool": to(offset)}, device_id_type=MESH,
        )

    def x_copy(offset):
        start = to(offset) * depth
        if share > 1:
            start = start + head * piece
        return pltpu.make_async_remote_copy(
            src_ref=hidden.at[:, pl.ds(pl.multiple_of(start, piece), piece)],
            dst_ref=x_in.at[offset, 0],
            send_sem=x_send.at[offset], recv_sem=x_recv.at[offset],
            device_id={"pool": to(offset)}, device_id_type=MESH,
        )

    def share_copy(offset, j):
        return pltpu.make_async_remote_copy(
            src_ref=x_in.at[offset, 0], dst_ref=x_in.at[offset, j],
            send_sem=f_send.at[offset, j], recv_sem=f_recv.at[offset, j],
            device_id={"head": lax.rem(head + j, heads)}, device_id_type=MESH,
        )

    def page_copy(offset):
        return pltpu.make_async_remote_copy(
            src_ref=page_out.at[offset], dst_ref=pages.at[offset],
            send_sem=g_send.at[offset], recv_sem=g_recv.at[offset],
            device_id={"pool": frm(offset)}, device_id_type=MESH,
        )

    def line_copy(bufs, t, going_right):
        out, scale, inbound, scale_in, send, recv = bufs
        side = 0 if going_right else 1
        peer = me + 1 if going_right else me - 1
        return [
            pltpu.make_async_remote_copy(
                src_ref=source.at[t], dst_ref=target.at[side, t],
                send_sem=send.at[k, t], recv_sem=recv.at[side, k, t],
                device_id={"pool": peer}, device_id_type=MESH,
            )
            for k, (source, target) in enumerate(((scale, scale_in), (out, inbound)))
        ]

    def fresh_copy(offset):
        return pltpu.make_async_remote_copy(
            src_ref=fresh, dst_ref=fresh_all.at[offset],
            send_sem=r_send.at[offset], recv_sem=r_recv.at[offset],
            device_id={"pool": to(offset)}, device_id_type=MESH,
        )

    def far_first(send, toward):
        @pl.loop(0, pool - 1)
        def _(step):
            distance = pool - 1 - step

            @pl.when(me + distance < pool)
            def _():
                send(distance if toward else pool - distance)

            @pl.when(me - distance >= 0)
            def _():
                send(pool - distance if toward else distance)

    def send_hidden(offset):
        meta_copy(offset).start()
        x_copy(offset).start()

    far_first(send_hidden, True)

    own_meta = pltpu.make_async_copy(meta.at[me], meta_all.at[0], own_sem.at[0])
    own_meta.start()
    loads[0].wait()
    for c in range(capacity):
        page_out[0, c] = store[own_pick[me, c]]
    own_pages = pltpu.make_async_copy(page_out.at[0], pages.at[0], own_sem.at[1])
    own_pages.start()

    def pick_copy(offset):
        return pltpu.make_async_copy(
            meta_all.at[offset, :, pl.ds(0, 128)], picks.at[offset], pick_sem.at[offset]
        )

    @pl.loop(1, pool)
    def _(offset):
        meta_copy(offset).wait_recv()
        pick_copy(offset).start()
        pick_copy(offset).wait()
        for c in range(capacity):
            page_out[offset, c] = store[picks[offset, 0, c]]
        page_copy(offset).start()

    for load in loads[1:]:
        load.wait()
    tile = 256 if q_cols % 256 == 0 and kv_cols % 256 == 0 else 128

    def project(target, x_of, weight, base):
        @pl.loop(0, weight.shape[1] // tile)
        def _(n):
            cols = pl.ds(pl.multiple_of(n * tile, tile), tile)
            total = None
            for x, start in x_of:
                term = jnp.dot(
                    x[...], weight[pl.ds(start, x.shape[1]), cols],
                    preferred_element_type=jnp.float32,
                )
                total = term if total is None else total + term
            target[:, pl.ds(pl.multiple_of(base + n * tile, tile), tile)] = total

    project(own_acc, [(own_x, 0)], wkv, q_cols)
    project(own_acc, [(own_x, 0)], wq, 0)

    if share > 1:
        def pass_on(offset):
            x_copy(offset).wait_recv()
            for j in range(1, share):
                share_copy(offset, j).start()

        far_first(pass_on, False)

    def encode(bufs, t, base, blocks):
        values = acc[:, base:base + blocks * 128]
        peak = jnp.max(jnp.abs(values), axis=1, keepdims=True)
        scale = jnp.broadcast_to(jnp.maximum(peak * 1.005, 1e-30), (rows, 128)).astype(jnp.bfloat16)
        bufs[1][t] = scale
        inverse = LEVELS / scale.astype(jnp.float32)
        for quad in range(0, blocks, 4):
            packed = jnp.full((rows, 128), -32768, jnp.int32)
            for n in range(quad, min(quad + 4, blocks)):
                code = jnp.round(acc[:, base + n * 128:base + (n + 1) * 128] * inverse).astype(jnp.int32)
                bufs[0][t, :, n * 128:(n + 1) * 128] = (code >> 4).astype(jnp.int16)
                packed = packed + ((code & 15) << (4 * (n - quad)))
            lane = (blocks + quad // 4) * 128
            bufs[0][t, :, lane:lane + 128] = packed.astype(jnp.int16)

    def add_in(target, bufs, t, side, base, blocks):
        for copy in line_copy(bufs, t, side == 0):
            copy.wait_recv()
        factor = bufs[3][side, t].astype(jnp.float32) * (1.0 / LEVELS)
        for quad in range(0, blocks, 4):
            lane = (blocks + quad // 4) * 128
            packed = bufs[2][side, t, :, lane:lane + 128].astype(jnp.int32) + 32768
            for n in range(quad, min(quad + 4, blocks)):
                high = bufs[2][side, t, :, n * 128:(n + 1) * 128].astype(jnp.int32)
                code = high * 16 + ((packed >> (4 * (n - quad))) & 15)
                target[:, base + n * 128:base + (n + 1) * 128] += code.astype(jnp.float32) * factor

    def reduce_line(bufs, weight, base, first):
        blocks = weight.shape[1] // 128

        def serve(t, going_right):
            slot = lax.rem(me - t + pool, pool)
            pieces = []
            for j in range(share):
                if first:
                    if j:
                        share_copy(slot, j).wait_recv()
                    elif share == 1:
                        x_copy(slot).wait_recv()
                start = pl.multiple_of(lax.rem(head + heads - j, heads) * piece, piece) if share > 1 else 0
                pieces.append((x_in.at[slot, j], start))
            project(acc, pieces, weight, base)
            side = 0 if going_right else 1

            @pl.when(me > 0 if going_right else me < pool - 1)
            def _():
                add_in(acc, bufs, t, side, base, blocks)

            encode(bufs, t, base, blocks)
            for copy in line_copy(bufs, t, going_right):
                copy.start()

        @pl.loop(0, pool - 1)
        def _(step):
            distance = pool - 1 - step

            @pl.when(me + distance < pool)
            def _():
                serve(me + distance, True)

            @pl.when(me - distance >= 0)
            def _():
                serve(me - distance, False)

        @pl.when(me > 0)
        def _():
            add_in(own_acc, bufs, me, 0, base, blocks)

        @pl.when(me < pool - 1)
        def _():
            add_in(own_acc, bufs, me, 1, base, blocks)

    def finish_line(bufs):
        @pl.loop(0, pool)
        def _(t):
            @pl.when(t > me)
            def _():
                for copy in line_copy(bufs, t, True):
                    copy.wait_send()

            @pl.when(t < me)
            def _():
                for copy in line_copy(bufs, t, False):
                    copy.wait_send()

    kv_bufs = (kv_out, kv_scale, kv_in, kv_scale_in, kv_send, kv_recv)
    q_bufs = (q_part, q_scale, q_in, q_scale_in, q_send, q_recv)
    reduce_line(kv_bufs, wkv, q_cols, True)

    def rotated(cols):
        value = own_acc[:, cols]
        return (value * cosine[...] + pltpu.roll(value, HD // 2, 1) * sine[...]).astype(jnp.bfloat16)

    for n in range(kv_cols // HD):
        cols = slice(q_cols + n * HD, q_cols + (n + 1) * HD)
        block = rotated(cols) if n % 2 == 0 else own_acc[:, cols].astype(jnp.bfloat16)
        fresh[:, n * HD:(n + 1) * HD] = block

    @pl.loop(1, pool)
    def _(offset):
        fresh_copy(offset).start()

    own_fresh = pltpu.make_async_copy(fresh, fresh_all.at[0], own_sem.at[2])
    own_fresh.start()
    reduce_line(q_bufs, wq, 0, False)
    for n in range(q_cols // HD):
        q_out[:, n * HD:(n + 1) * HD] = rotated(slice(n * HD, (n + 1) * HD))

    own_meta.wait()
    own_pages.wait()
    own_fresh.wait()

    @pl.loop(1, pool)
    def _(offset):
        fresh_copy(offset).wait_recv()
        page_copy(offset).wait_recv()
        meta_copy(offset).wait_send()
        x_copy(offset).wait_send()
        for j in range(1, share):
            share_copy(offset, j).wait_send()
        page_copy(offset).wait_send()
        fresh_copy(offset).wait_send()

    finish_line(kv_bufs)
    finish_line(q_bufs)


def attend_kernel(
    pool,
    gather, q, fresh_all, pages, meta_all, store, pos_row,
    attended, new_store,
    context,
):
    sessions, context_pages = gather.shape
    page_len, width = store.shape[1:]
    context_len = context_pages * page_len
    rows, q_cols = q.shape
    pick = rows // sessions
    local_kv = width // (2 * HD)
    group = q_cols // HD // local_kv
    for s in range(sessions):
        @pl.loop(0, context_pages)
        def _(p):
            context[pl.ds(pl.multiple_of(p * page_len, page_len), page_len), :] = pages[gather[s, p]]

        token = lax.broadcasted_iota(jnp.int32, (context_len, pick), 0)
        hot = jnp.where(token == pos_row[s], 1.0, 0.0).astype(jnp.bfloat16)
        taken = jnp.dot(hot, jnp.ones((pick, HD), jnp.bfloat16), preferred_element_type=jnp.float32) > 0.5
        mine = fresh_all[0, s * pick:(s + 1) * pick, :]
        for n in range(width // HD):
            cols = slice(n * HD, (n + 1) * HD)
            spread = jnp.dot(hot, mine[:, cols], preferred_element_type=jnp.float32)
            context[:, cols] = jnp.where(
                taken, spread, context[:, cols].astype(jnp.float32)
            ).astype(jnp.bfloat16)
        diagonal = lax.broadcasted_iota(jnp.int32, (pick, pick), 0) == lax.broadcasted_iota(
            jnp.int32, (pick, pick), 1
        )
        spot = jnp.sum(
            jnp.where(diagonal, pos_row[s].astype(jnp.float32), 0.0), axis=1, keepdims=True
        ).astype(jnp.int32)
        limit = jnp.concatenate([spot] * group, axis=0)
        column = lax.broadcasted_iota(jnp.int32, (group * pick, context_len), 1)
        allowed = column <= limit
        for k in range(local_kv):
            keys = context[:, 2 * k * HD:(2 * k + 1) * HD]
            vals = context[:, (2 * k + 1) * HD:(2 * k + 2) * HD]
            heads = jnp.concatenate(
                [
                    q[s * pick:(s + 1) * pick, (k * group + g) * HD:(k * group + g + 1) * HD]
                    for g in range(group)
                ],
                axis=0,
            )
            scores = lax.dot_general(
                heads, keys, (((1,), (1,)), ((), ())), preferred_element_type=jnp.float32
            ) * (1.0 / math.sqrt(HD))
            scores = jnp.where(allowed, scores, -jnp.inf)
            exps = jnp.exp(scores - jnp.max(scores, axis=1, keepdims=True))
            weights = (exps * (1.0 / jnp.sum(exps, axis=1, keepdims=True))).astype(jnp.bfloat16)
            out = jnp.dot(weights, vals, preferred_element_type=jnp.float32).astype(jnp.bfloat16)
            for g in range(group):
                attended[s * pick:(s + 1) * pick, (k * group + g) * HD:(k * group + g + 1) * HD] = (
                    out[g * pick:(g + 1) * pick]
                )

    held = store.shape[0]
    chunk = next(c for c in (8, 6, 4, 3, 2, 1) if held % c == 0)
    span = chunk * page_len

    @pl.loop(0, held // chunk)
    def _(b):
        slots = pl.ds(b * chunk, chunk)
        place = lax.axis_index("pool") * held * page_len + b * span + lax.broadcasted_iota(jnp.int32, (span, rows), 0)
        ones = jnp.ones((rows, HD), jnp.bfloat16)

        def add(offset, carry):
            total, count = carry
            goal = meta_all[offset, 1:2, 0:rows]
            hot = jnp.where(place == goal, 1.0, 0.0).astype(jnp.bfloat16)
            total = total + jnp.dot(hot, fresh_all[offset], preferred_element_type=jnp.float32)
            count = count + jnp.dot(hot, ones, preferred_element_type=jnp.float32)
            return total, count

        total, count = lax.fori_loop(
            0, pool, add,
            (jnp.zeros((span, width), jnp.float32), jnp.zeros((span, HD), jnp.float32)),
        )
        taken = count > 0.5
        for n in range(width // HD):
            cols = slice(n * HD, (n + 1) * HD)
            old = store[slots, :, cols].reshape(span, HD).astype(jnp.float32)
            new = jnp.where(taken, total[:, cols], old).astype(jnp.bfloat16)
            new_store[slots, :, cols] = new.reshape(chunk, page_len, HD)


def body(hidden, select, page_table, kv_store, w_query, w_kv):
    rows = hidden.shape[0]
    sessions, pick_count = select.shape
    held_slots, page_len, width = kv_store.shape
    depth, q_cols = w_query.shape
    kv_cols = w_kv.shape[1]
    pool = lax.axis_size("pool")
    heads = lax.axis_size("head")
    me = lax.axis_index("pool")
    share = heads if depth % (128 * heads) == 0 else 1
    context_pages = page_table.shape[1]
    entry_count = sessions * context_pages
    capacity = max(2, 2 * ((entry_count + 2 * pool - 1) // (2 * pool)))
    lanes = 128 * ((max(rows, capacity) + 127) // 128)

    positions = select.reshape(rows)
    half = HD // 2
    freqs = jnp.power(jnp.float32(ROPE_BASE), -(jnp.arange(half, dtype=jnp.float32) * 2.0 / HD))
    angles = positions.astype(jnp.float32)[:, None] * freqs[None, :]
    cosine = jnp.cos(angles)
    sine = jnp.sin(angles)
    cosine = jnp.concatenate([cosine, cosine], axis=1)
    sine = jnp.concatenate([-sine, sine], axis=1)

    table = page_table.reshape(entry_count)
    is_live, holder_of, rank_of = holder_rank(table, held_slots)
    target = jnp.where(is_live, holder_of * capacity + rank_of, -1)
    own_slots = table % held_slots
    request = jnp.max(
        jnp.where(target[:, None] == jnp.arange(pool * capacity)[None, :], own_slots[:, None], 0),
        axis=0,
    ).reshape(pool, capacity).astype(jnp.int32)
    page_of = select // page_len
    slot_of = jnp.max(
        jnp.where(page_of[:, :, None] == jnp.arange(context_pages)[None, None], page_table[:, None, :], -1),
        axis=2,
    )
    goal = (slot_of * page_len + select % page_len).reshape(1, rows)
    meta = jnp.concatenate(
        [
            jnp.pad(request, ((0, 0), (0, lanes - capacity)))[:, None, :],
            jnp.broadcast_to(jnp.pad(goal, ((0, 0), (0, lanes - rows)))[None], (pool, 1, lanes)),
            jnp.zeros((pool, 6, lanes), jnp.int32),
        ],
        axis=1,
    ).astype(jnp.int32)
    relative = jnp.where(is_live, (holder_of - me + pool) % pool, 0)
    gather = jnp.where(is_live, relative * capacity + rank_of, 0).reshape(sessions, context_pages)
    gather = gather.astype(jnp.int32)

    bf16, f32, i32 = jnp.bfloat16, jnp.float32, jnp.int32
    cols = q_cols + kv_cols
    dma = pltpu.SemaphoreType.DMA

    def line_scratch(width):
        coded = width + 128 * ((width // 128 + 3) // 4)
        return (
            pltpu.VMEM((pool, rows, coded), jnp.int16),
            pltpu.VMEM((pool, rows, 128), bf16),
            pltpu.VMEM((2, pool, rows, coded), jnp.int16),
            pltpu.VMEM((2, pool, rows, 128), bf16),
        )

    q, fresh_all, pages, meta_all = pl.pallas_call(
        functools.partial(exchange_kernel, pool, heads, share, capacity),
        out_shape=(
            jax.ShapeDtypeStruct((rows, q_cols), bf16),
            jax.ShapeDtypeStruct((pool, rows, kv_cols), bf16),
            jax.ShapeDtypeStruct((pool, capacity, page_len, width), bf16),
            jax.ShapeDtypeStruct((pool, 8, lanes), i32),
        ),
        in_specs=[ANY, ANY, ANY, ANY, ANY, SMEM, VMEM, VMEM],
        out_specs=(VMEM, ANY, ANY, ANY),
        scratch_shapes=[
            pltpu.VMEM((depth, q_cols), bf16),
            pltpu.VMEM((depth, kv_cols), bf16),
            pltpu.VMEM((held_slots, page_len, width), bf16),
            pltpu.VMEM((rows, depth), bf16),
            pltpu.VMEM((pool, share, rows, depth // share), bf16),
            pltpu.VMEM((rows, cols), f32),
            pltpu.VMEM((rows, cols), f32),
            *line_scratch(kv_cols),
            *line_scratch(q_cols),
            pltpu.VMEM((pool, capacity, page_len, width), bf16),
            pltpu.VMEM((rows, kv_cols), bf16),
            pltpu.SMEM((pool, 8, 128), i32),
            dma((4,)),
            dma((pool,)), dma((pool,)),
            dma((pool, share)), dma((pool, share)),
            dma((pool,)), dma((pool,)), dma((pool,)),
            dma((pool,)), dma((pool,)),
            dma((2, pool)), dma((2, 2, pool)),
            dma((2, pool)), dma((2, 2, pool)),
            dma((pool,)), dma((pool,)),
            dma((3,)),
        ],
        compiler_params=pltpu.CompilerParams(
            collective_id=0, has_side_effects=True, vmem_limit_bytes=VMEM_BYTES
        ),
    )(meta, hidden, w_query, w_kv, kv_store, request, cosine, sine)

    attended, new_store = pl.pallas_call(
        functools.partial(attend_kernel, pool),
        out_shape=(
            jax.ShapeDtypeStruct((rows, q_cols), bf16),
            jax.ShapeDtypeStruct(kv_store.shape, bf16),
        ),
        in_specs=[SMEM] + [VMEM] * 6,
        out_specs=(VMEM, VMEM),
        scratch_shapes=[pltpu.VMEM((context_pages * page_len, width), bf16)],
        compiler_params=pltpu.CompilerParams(vmem_limit_bytes=VMEM_BYTES),
    )(
        gather, q, fresh_all,
        pages.reshape(pool * capacity, page_len, width), meta_all, kv_store,
        select.reshape(sessions, 1, pick_count),
    )
    return attended, new_store


def solution(mesh):
    return jax.shard_map(
        body,
        mesh=mesh,
        in_specs=(
            P(("groups", "pool"), None),
            P(("groups", "pool"), None),
            P(("groups", "pool"), None),
            P(("groups", "pool"), None, "head"),
            P("pool", "head"),
            P("pool", "head"),
        ),
        out_specs=(P(("groups", "pool"), "head"), P(("groups", "pool"), None, "head")),
        check_vma=False,
    )
```

```python
import functools
import math

import jax
import jax.numpy as jnp
from jax import lax
from jax.experimental import pallas as pl
from jax.experimental.pallas import tpu as pltpu
from jax.sharding import PartitionSpec as P

HD = 128
ROPE_BASE = 500000.0
MESH = pl.DeviceIdType.MESH
ANY = pl.BlockSpec(memory_space=pl.ANY)
VMEM = pl.BlockSpec(memory_space=pltpu.VMEM)
SMEM = pl.BlockSpec(memory_space=pltpu.SMEM)
LEVELS = 519000.0
VMEM_BYTES = 56 * 1024 * 1024


def holder_rank(table_rows, held_slots):
    is_live = table_rows >= 0
    holder_of = jnp.where(is_live, table_rows // held_slots, -1)
    entry_count = table_rows.shape[0]
    earlier = jnp.arange(entry_count)[None, :] < jnp.arange(entry_count)[:, None]
    same = (holder_of[:, None] == holder_of[None, :]) & earlier & is_live[None, :]
    return is_live, holder_of, jnp.sum(same, axis=1)


def exchange_kernel(
    pool, heads, share, capacity,
    meta, hidden, wq_hbm, wkv_hbm, store_hbm, own_pick, cosine, sine,
    q_out, fresh_all, pages, meta_all,
    wq, wkv, store, own_x, x_in, acc, own_acc, kv_out, kv_scale, kv_in, kv_scale_in, q_part, q_scale, q_in, q_scale_in,
    page_out, fresh,
    picks,
    load_sem, x_send, x_recv, f_send, f_recv, m_send, m_recv, pick_sem,
    g_send, g_recv, kv_send, kv_recv, q_send, q_recv, r_send, r_recv, own_sem,
):
    me = lax.axis_index("pool")
    head = lax.axis_index("head")
    depth, q_cols = wq.shape
    kv_cols = wkv.shape[1]
    rows = hidden.shape[0]
    piece = depth // share

    def to(offset):
        return lax.rem(me + offset, pool)

    def frm(offset):
        return lax.rem(me + pool - offset, pool)

    loads = [
        pltpu.make_async_copy(store_hbm, store, load_sem.at[0]),
        pltpu.make_async_copy(
            hidden.at[:, pl.ds(pl.multiple_of(me * depth, depth), depth)], own_x, load_sem.at[1]
        ),
        pltpu.make_async_copy(wq_hbm, wq, load_sem.at[2]),
        pltpu.make_async_copy(wkv_hbm, wkv, load_sem.at[3]),
    ]
    for load in loads:
        load.start()

    barrier = pltpu.get_barrier_semaphore()

    @pl.loop(1, pool)
    def _(offset):
        pl.semaphore_signal(barrier, inc=1, device_id={"pool": to(offset)}, device_id_type=MESH)

    for j in range(1, share):
        pl.semaphore_signal(
            barrier, inc=1, device_id={"head": lax.rem(head + j, heads)}, device_id_type=MESH
        )
    pl.semaphore_wait(barrier, pool - 1 + share - 1)

    def meta_copy(offset):
        return pltpu.make_async_remote_copy(
            src_ref=meta.at[to(offset)], dst_ref=meta_all.at[offset],
            send_sem=m_send.at[offset], recv_sem=m_recv.at[offset],
            device_id={"pool": to(offset)}, device_id_type=MESH,
        )

    def x_copy(offset):
        start = to(offset) * depth
        if share > 1:
            start = start + head * piece
        return pltpu.make_async_remote_copy(
            src_ref=hidden.at[:, pl.ds(pl.multiple_of(start, piece), piece)],
            dst_ref=x_in.at[offset, 0],
            send_sem=x_send.at[offset], recv_sem=x_recv.at[offset],
            device_id={"pool": to(offset)}, device_id_type=MESH,
        )

    def share_copy(offset, j):
        return pltpu.make_async_remote_copy(
            src_ref=x_in.at[offset, 0], dst_ref=x_in.at[offset, j],
            send_sem=f_send.at[offset, j], recv_sem=f_recv.at[offset, j],
            device_id={"head": lax.rem(head + j, heads)}, device_id_type=MESH,
        )

    def page_copy(offset):
        return pltpu.make_async_remote_copy(
            src_ref=page_out.at[offset], dst_ref=pages.at[offset],
            send_sem=g_send.at[offset], recv_sem=g_recv.at[offset],
            device_id={"pool": frm(offset)}, device_id_type=MESH,
        )

    def line_copy(bufs, t, going_right):
        out, scale, inbound, scale_in, send, recv = bufs
        side = 0 if going_right else 1
        peer = me + 1 if going_right else me - 1
        return [
            pltpu.make_async_remote_copy(
                src_ref=source.at[t], dst_ref=target.at[side, t],
                send_sem=send.at[k, t], recv_sem=recv.at[side, k, t],
                device_id={"pool": peer}, device_id_type=MESH,
            )
            for k, (source, target) in enumerate(((scale, scale_in), (out, inbound)))
        ]

    def fresh_copy(offset):
        return pltpu.make_async_remote_copy(
            src_ref=fresh, dst_ref=fresh_all.at[offset],
            send_sem=r_send.at[offset], recv_sem=r_recv.at[offset],
            device_id={"pool": to(offset)}, device_id_type=MESH,
        )

    def far_first(send, toward):
        @pl.loop(0, pool - 1)
        def _(step):
            distance = pool - 1 - step

            @pl.when(me + distance < pool)
            def _():
                send(distance if toward else pool - distance)

            @pl.when(me - distance >= 0)
            def _():
                send(pool - distance if toward else distance)

    def send_hidden(offset):
        meta_copy(offset).start()
        x_copy(offset).start()

    far_first(send_hidden, True)

    own_meta = pltpu.make_async_copy(meta.at[me], meta_all.at[0], own_sem.at[0])
    own_meta.start()
    loads[0].wait()
    for c in range(capacity):
        page_out[0, c] = store[own_pick[me, c]]
    own_pages = pltpu.make_async_copy(page_out.at[0], pages.at[0], own_sem.at[1])
    own_pages.start()

    def pick_copy(offset):
        return pltpu.make_async_copy(
            meta_all.at[offset, :, pl.ds(0, 128)], picks.at[offset], pick_sem.at[offset]
        )

    @pl.loop(1, pool)
    def _(offset):
        meta_copy(offset).wait_recv()
        pick_copy(offset).start()
        pick_copy(offset).wait()
        for c in range(capacity):
            page_out[offset, c] = store[picks[offset, 0, c]]
        page_copy(offset).start()

    for load in loads[1:]:
        load.wait()
    tile = 256 if q_cols % 256 == 0 and kv_cols % 256 == 0 else 128

    def project(target, x_of, weight, base):
        @pl.loop(0, weight.shape[1] // tile)
        def _(n):
            cols = pl.ds(pl.multiple_of(n * tile, tile), tile)
            total = None
            for x, start in x_of:
                term = jnp.dot(
                    x[...], weight[pl.ds(start, x.shape[1]), cols],
                    preferred_element_type=jnp.float32,
                )
                total = term if total is None else total + term
            target[:, pl.ds(pl.multiple_of(base + n * tile, tile), tile)] = total

    project(own_acc, [(own_x, 0)], wkv, q_cols)
    project(own_acc, [(own_x, 0)], wq, 0)

    if share > 1:
        def pass_on(offset):
            x_copy(offset).wait_recv()
            for j in range(1, share):
                share_copy(offset, j).start()

        far_first(pass_on, False)

    def encode(bufs, t, base, blocks):
        values = acc[:, base:base + blocks * 128]
        peak = jnp.max(jnp.abs(values), axis=1, keepdims=True)
        scale = jnp.broadcast_to(jnp.maximum(peak * 1.005, 1e-30), (rows, 128)).astype(jnp.bfloat16)
        bufs[1][t] = scale
        inverse = LEVELS / scale.astype(jnp.float32)
        for quad in range(0, blocks, 4):
            packed = jnp.full((rows, 128), -32768, jnp.int32)
            for n in range(quad, min(quad + 4, blocks)):
                code = jnp.round(acc[:, base + n * 128:base + (n + 1) * 128] * inverse).astype(jnp.int32)
                bufs[0][t, :, n * 128:(n + 1) * 128] = (code >> 4).astype(jnp.int16)
                packed = packed + ((code & 15) << (4 * (n - quad)))
            lane = (blocks + quad // 4) * 128
            bufs[0][t, :, lane:lane + 128] = packed.astype(jnp.int16)

    def add_in(target, bufs, t, side, base, blocks):
        for copy in line_copy(bufs, t, side == 0):
            copy.wait_recv()
        factor = bufs[3][side, t].astype(jnp.float32) * (1.0 / LEVELS)
        for quad in range(0, blocks, 4):
            lane = (blocks + quad // 4) * 128
            packed = bufs[2][side, t, :, lane:lane + 128].astype(jnp.int32) + 32768
            for n in range(quad, min(quad + 4, blocks)):
                high = bufs[2][side, t, :, n * 128:(n + 1) * 128].astype(jnp.int32)
                code = high * 16 + ((packed >> (4 * (n - quad))) & 15)
                target[:, base + n * 128:base + (n + 1) * 128] += code.astype(jnp.float32) * factor

    def reduce_line(bufs, weight, base, first):
        blocks = weight.shape[1] // 128

        def serve(t, going_right):
            slot = lax.rem(me - t + pool, pool)
            pieces = []
            for j in range(share):
                if first:
                    if j:
                        share_copy(slot, j).wait_recv()
                    elif share == 1:
                        x_copy(slot).wait_recv()
                start = pl.multiple_of(lax.rem(head + heads - j, heads) * piece, piece) if share > 1 else 0
                pieces.append((x_in.at[slot, j], start))
            project(acc, pieces, weight, base)
            side = 0 if going_right else 1

            @pl.when(me > 0 if going_right else me < pool - 1)
            def _():
                add_in(acc, bufs, t, side, base, blocks)

            encode(bufs, t, base, blocks)
            for copy in line_copy(bufs, t, going_right):
                copy.start()

        @pl.loop(0, pool - 1)
        def _(step):
            distance = pool - 1 - step

            @pl.when(me + distance < pool)
            def _():
                serve(me + distance, True)

            @pl.when(me - distance >= 0)
            def _():
                serve(me - distance, False)

        @pl.when(me > 0)
        def _():
            add_in(own_acc, bufs, me, 0, base, blocks)

        @pl.when(me < pool - 1)
        def _():
            add_in(own_acc, bufs, me, 1, base, blocks)

    def finish_line(bufs):
        @pl.loop(0, pool)
        def _(t):
            @pl.when(t > me)
            def _():
                for copy in line_copy(bufs, t, True):
                    copy.wait_send()

            @pl.when(t < me)
            def _():
                for copy in line_copy(bufs, t, False):
                    copy.wait_send()

    kv_bufs = (kv_out, kv_scale, kv_in, kv_scale_in, kv_send, kv_recv)
    q_bufs = (q_part, q_scale, q_in, q_scale_in, q_send, q_recv)
    reduce_line(kv_bufs, wkv, q_cols, True)

    def rotated(cols):
        value = own_acc[:, cols]
        return (value * cosine[...] + pltpu.roll(value, HD // 2, 1) * sine[...]).astype(jnp.bfloat16)

    for n in range(kv_cols // HD):
        cols = slice(q_cols + n * HD, q_cols + (n + 1) * HD)
        block = rotated(cols) if n % 2 == 0 else own_acc[:, cols].astype(jnp.bfloat16)
        fresh[:, n * HD:(n + 1) * HD] = block

    @pl.loop(1, pool)
    def _(offset):
        fresh_copy(offset).start()

    own_fresh = pltpu.make_async_copy(fresh, fresh_all.at[0], own_sem.at[2])
    own_fresh.start()
    reduce_line(q_bufs, wq, 0, False)
    for n in range(q_cols // HD):
        q_out[:, n * HD:(n + 1) * HD] = rotated(slice(n * HD, (n + 1) * HD))

    own_meta.wait()
    own_pages.wait()
    own_fresh.wait()

    @pl.loop(1, pool)
    def _(offset):
        fresh_copy(offset).wait_recv()
        page_copy(offset).wait_recv()
        meta_copy(offset).wait_send()
        x_copy(offset).wait_send()
        for j in range(1, share):
            share_copy(offset, j).wait_send()
        page_copy(offset).wait_send()
        fresh_copy(offset).wait_send()

    finish_line(kv_bufs)
    finish_line(q_bufs)


def attend_kernel(
    pool,
    gather, q, fresh_all, pages, goals, store, pos_row,
    attended, new_store,
    context,
):
    sessions, context_pages = gather.shape
    page_len, width = store.shape[1:]
    context_len = context_pages * page_len
    rows, q_cols = q.shape
    pick = rows // sessions
    local_kv = width // (2 * HD)
    group = q_cols // HD // local_kv
    for s in range(sessions):
        @pl.loop(0, context_pages)
        def _(p):
            context[pl.ds(pl.multiple_of(p * page_len, page_len), page_len), :] = pages[gather[s, p]]

        token = lax.broadcasted_iota(jnp.int32, (context_len, pick), 0)
        hot = jnp.where(token == pos_row[s], 1.0, 0.0).astype(jnp.bfloat16)
        taken = jnp.dot(hot, jnp.ones((pick, HD), jnp.bfloat16), preferred_element_type=jnp.float32) > 0.5
        mine = fresh_all[s * pick:(s + 1) * pick, :]
        for n in range(width // HD):
            cols = slice(n * HD, (n + 1) * HD)
            spread = jnp.dot(hot, mine[:, cols], preferred_element_type=jnp.float32)
            context[:, cols] = jnp.where(
                taken, spread, context[:, cols].astype(jnp.float32)
            ).astype(jnp.bfloat16)
        diagonal = lax.broadcasted_iota(jnp.int32, (pick, pick), 0) == lax.broadcasted_iota(
            jnp.int32, (pick, pick), 1
        )
        spot = jnp.sum(
            jnp.where(diagonal, pos_row[s].astype(jnp.float32), 0.0), axis=1, keepdims=True
        ).astype(jnp.int32)
        limit = jnp.concatenate([spot] * group, axis=0)
        column = lax.broadcasted_iota(jnp.int32, (group * pick, context_len), 1)
        allowed = column <= limit
        for k in range(local_kv):
            keys = context[:, 2 * k * HD:(2 * k + 1) * HD]
            vals = context[:, (2 * k + 1) * HD:(2 * k + 2) * HD]
            heads = jnp.concatenate(
                [
                    q[s * pick:(s + 1) * pick, (k * group + g) * HD:(k * group + g + 1) * HD]
                    for g in range(group)
                ],
                axis=0,
            )
            scores = lax.dot_general(
                heads, keys, (((1,), (1,)), ((), ())), preferred_element_type=jnp.float32
            ) * (1.0 / math.sqrt(HD))
            scores = jnp.where(allowed, scores, -jnp.inf)
            exps = jnp.exp(scores - jnp.max(scores, axis=1, keepdims=True))
            weights = (exps * (1.0 / jnp.sum(exps, axis=1, keepdims=True))).astype(jnp.bfloat16)
            out = jnp.dot(weights, vals, preferred_element_type=jnp.float32).astype(jnp.bfloat16)
            for g in range(group):
                attended[s * pick:(s + 1) * pick, (k * group + g) * HD:(k * group + g + 1) * HD] = (
                    out[g * pick:(g + 1) * pick]
                )

    held = store.shape[0]
    chunk = next(c for c in (8, 6, 4, 3, 2, 1) if held % c == 0)
    span = chunk * page_len

    @pl.loop(0, held // chunk)
    def _(b):
        slots = pl.ds(b * chunk, chunk)
        first = lax.axis_index("pool") * held * page_len + b * span
        place = first + lax.broadcasted_iota(jnp.int32, (span, pool * rows), 0)
        hot = jnp.where(place == goals[...], 1.0, 0.0).astype(jnp.bfloat16)
        count = jnp.dot(
            hot, jnp.ones((pool * rows, HD), jnp.bfloat16), preferred_element_type=jnp.float32
        )
        taken = count > 0.5
        for n in range(width // HD):
            cols = slice(n * HD, (n + 1) * HD)
            old = store[slots, :, cols].reshape(span, HD).astype(jnp.float32)
            total = jnp.dot(hot, fresh_all[:, cols], preferred_element_type=jnp.float32)
            new = jnp.where(taken, total, old).astype(jnp.bfloat16)
            new_store[slots, :, cols] = new.reshape(chunk, page_len, HD)


def body(hidden, select, page_table, kv_store, w_query, w_kv):
    rows = hidden.shape[0]
    sessions, pick_count = select.shape
    held_slots, page_len, width = kv_store.shape
    depth, q_cols = w_query.shape
    kv_cols = w_kv.shape[1]
    pool = lax.axis_size("pool")
    heads = lax.axis_size("head")
    me = lax.axis_index("pool")
    share = heads if depth % (128 * heads) == 0 else 1
    context_pages = page_table.shape[1]
    entry_count = sessions * context_pages
    capacity = max(2, 2 * ((entry_count + 2 * pool - 1) // (2 * pool)))
    lanes = 128 * ((max(rows, capacity) + 127) // 128)

    positions = select.reshape(rows)
    half = HD // 2
    freqs = jnp.power(jnp.float32(ROPE_BASE), -(jnp.arange(half, dtype=jnp.float32) * 2.0 / HD))
    angles = positions.astype(jnp.float32)[:, None] * freqs[None, :]
    cosine = jnp.cos(angles)
    sine = jnp.sin(angles)
    cosine = jnp.concatenate([cosine, cosine], axis=1)
    sine = jnp.concatenate([-sine, sine], axis=1)

    table = page_table.reshape(entry_count)
    is_live, holder_of, rank_of = holder_rank(table, held_slots)
    target = jnp.where(is_live, holder_of * capacity + rank_of, -1)
    own_slots = table % held_slots
    request = jnp.max(
        jnp.where(target[:, None] == jnp.arange(pool * capacity)[None, :], own_slots[:, None], 0),
        axis=0,
    ).reshape(pool, capacity).astype(jnp.int32)
    page_of = select // page_len
    slot_of = jnp.max(
        jnp.where(page_of[:, :, None] == jnp.arange(context_pages)[None, None], page_table[:, None, :], -1),
        axis=2,
    )
    goal = (slot_of * page_len + select % page_len).reshape(1, rows)
    meta = jnp.concatenate(
        [
            jnp.pad(request, ((0, 0), (0, lanes - capacity)))[:, None, :],
            jnp.broadcast_to(jnp.pad(goal, ((0, 0), (0, lanes - rows)))[None], (pool, 1, lanes)),
            jnp.zeros((pool, 6, lanes), jnp.int32),
        ],
        axis=1,
    ).astype(jnp.int32)
    relative = jnp.where(is_live, (holder_of - me + pool) % pool, 0)
    gather = jnp.where(is_live, relative * capacity + rank_of, 0).reshape(sessions, context_pages)
    gather = gather.astype(jnp.int32)

    bf16, f32, i32 = jnp.bfloat16, jnp.float32, jnp.int32
    cols = q_cols + kv_cols
    dma = pltpu.SemaphoreType.DMA

    def line_scratch(width):
        coded = width + 128 * ((width // 128 + 3) // 4)
        return (
            pltpu.VMEM((pool, rows, coded), jnp.int16),
            pltpu.VMEM((pool, rows, 128), bf16),
            pltpu.VMEM((2, pool, rows, coded), jnp.int16),
            pltpu.VMEM((2, pool, rows, 128), bf16),
        )

    q, fresh_all, pages, meta_all = pl.pallas_call(
        functools.partial(exchange_kernel, pool, heads, share, capacity),
        out_shape=(
            jax.ShapeDtypeStruct((rows, q_cols), bf16),
            jax.ShapeDtypeStruct((pool, rows, kv_cols), bf16),
            jax.ShapeDtypeStruct((pool, capacity, page_len, width), bf16),
            jax.ShapeDtypeStruct((pool, 8, lanes), i32),
        ),
        in_specs=[ANY, ANY, ANY, ANY, ANY, SMEM, VMEM, VMEM],
        out_specs=(VMEM, ANY, ANY, ANY),
        scratch_shapes=[
            pltpu.VMEM((depth, q_cols), bf16),
            pltpu.VMEM((depth, kv_cols), bf16),
            pltpu.VMEM((held_slots, page_len, width), bf16),
            pltpu.VMEM((rows, depth), bf16),
            pltpu.VMEM((pool, share, rows, depth // share), bf16),
            pltpu.VMEM((rows, cols), f32),
            pltpu.VMEM((rows, cols), f32),
            *line_scratch(kv_cols),
            *line_scratch(q_cols),
            pltpu.VMEM((pool, capacity, page_len, width), bf16),
            pltpu.VMEM((rows, kv_cols), bf16),
            pltpu.SMEM((pool, 8, 128), i32),
            dma((4,)),
            dma((pool,)), dma((pool,)),
            dma((pool, share)), dma((pool, share)),
            dma((pool,)), dma((pool,)), dma((pool,)),
            dma((pool,)), dma((pool,)),
            dma((2, pool)), dma((2, 2, pool)),
            dma((2, pool)), dma((2, 2, pool)),
            dma((pool,)), dma((pool,)),
            dma((3,)),
        ],
        compiler_params=pltpu.CompilerParams(
            collective_id=0, has_side_effects=True, vmem_limit_bytes=VMEM_BYTES
        ),
    )(meta, hidden, w_query, w_kv, kv_store, request, cosine, sine)

    goals = meta_all[:, 1, :rows].reshape(1, pool * rows)
    attended, new_store = pl.pallas_call(
        functools.partial(attend_kernel, pool),
        out_shape=(
            jax.ShapeDtypeStruct((rows, q_cols), bf16),
            jax.ShapeDtypeStruct(kv_store.shape, bf16),
        ),
        in_specs=[SMEM] + [VMEM] * 6,
        out_specs=(VMEM, VMEM),
        scratch_shapes=[pltpu.VMEM((context_pages * page_len, width), bf16)],
        compiler_params=pltpu.CompilerParams(vmem_limit_bytes=VMEM_BYTES),
    )(
        gather, q, fresh_all.reshape(pool * rows, kv_cols),
        pages.reshape(pool * capacity, page_len, width), goals, kv_store,
        select.reshape(sessions, 1, pick_count),
    )
    return attended, new_store


def solution(mesh):
    return jax.shard_map(
        body,
        mesh=mesh,
        in_specs=(
            P(("groups", "pool"), None),
            P(("groups", "pool"), None),
            P(("groups", "pool"), None),
            P(("groups", "pool"), None, "head"),
            P("pool", "head"),
            P("pool", "head"),
        ),
        out_specs=(P(("groups", "pool"), "head"), P(("groups", "pool"), None, "head")),
        check_vma=False,
    )
```

```python
import functools
import math

import jax
import jax.numpy as jnp
from jax import lax
from jax.experimental import pallas as pl
from jax.experimental.pallas import tpu as pltpu
from jax.sharding import PartitionSpec as P

HD = 128
ROPE_BASE = 500000.0
MESH = pl.DeviceIdType.MESH
ANY = pl.BlockSpec(memory_space=pl.ANY)
VMEM = pl.BlockSpec(memory_space=pltpu.VMEM)
SMEM = pl.BlockSpec(memory_space=pltpu.SMEM)
LEVELS = 519000.0
VMEM_BYTES = 56 * 1024 * 1024


def holder_rank(table_rows, held_slots):
    is_live = table_rows >= 0
    holder_of = jnp.where(is_live, table_rows // held_slots, -1)
    entry_count = table_rows.shape[0]
    earlier = jnp.arange(entry_count)[None, :] < jnp.arange(entry_count)[:, None]
    same = (holder_of[:, None] == holder_of[None, :]) & earlier & is_live[None, :]
    return is_live, holder_of, jnp.sum(same, axis=1)


def exchange_kernel(
    pool, heads, share, capacity,
    meta, hidden, wq_hbm, wkv_hbm, store_hbm, own_pick, cosine, sine,
    q_out, fresh_all, pages, meta_all,
    wq, wkv, store, own_x, x_in, acc, own_acc, kv_out, kv_scale, kv_in, kv_scale_in, q_part, q_scale, q_in, q_scale_in,
    page_out, fresh,
    picks,
    load_sem, x_send, x_recv, f_send, f_recv, m_send, m_recv, pick_sem,
    g_send, g_recv, kv_send, kv_recv, q_send, q_recv, r_send, r_recv, own_sem,
):
    me = lax.axis_index("pool")
    head = lax.axis_index("head")
    depth, q_cols = wq.shape
    kv_cols = wkv.shape[1]
    rows = hidden.shape[0]
    piece = depth // share

    def to(offset):
        return lax.rem(me + offset, pool)

    def frm(offset):
        return lax.rem(me + pool - offset, pool)

    loads = [
        pltpu.make_async_copy(store_hbm, store, load_sem.at[0]),
        pltpu.make_async_copy(
            hidden.at[:, pl.ds(pl.multiple_of(me * depth, depth), depth)], own_x, load_sem.at[1]
        ),
        pltpu.make_async_copy(wq_hbm, wq, load_sem.at[2]),
        pltpu.make_async_copy(wkv_hbm, wkv, load_sem.at[3]),
    ]
    for load in loads:
        load.start()

    barrier = pltpu.get_barrier_semaphore()

    @pl.loop(1, pool)
    def _(offset):
        pl.semaphore_signal(barrier, inc=1, device_id={"pool": to(offset)}, device_id_type=MESH)

    for j in range(1, share):
        pl.semaphore_signal(
            barrier, inc=1, device_id={"head": lax.rem(head + j, heads)}, device_id_type=MESH
        )
    pl.semaphore_wait(barrier, pool - 1 + share - 1)

    def meta_copy(offset):
        return pltpu.make_async_remote_copy(
            src_ref=meta.at[to(offset)], dst_ref=meta_all.at[offset],
            send_sem=m_send.at[offset], recv_sem=m_recv.at[offset],
            device_id={"pool": to(offset)}, device_id_type=MESH,
        )

    def x_copy(offset):
        start = to(offset) * depth
        if share > 1:
            start = start + head * piece
        return pltpu.make_async_remote_copy(
            src_ref=hidden.at[:, pl.ds(pl.multiple_of(start, piece), piece)],
            dst_ref=x_in.at[offset, 0],
            send_sem=x_send.at[offset], recv_sem=x_recv.at[offset],
            device_id={"pool": to(offset)}, device_id_type=MESH,
        )

    def share_copy(offset, j):
        return pltpu.make_async_remote_copy(
            src_ref=x_in.at[offset, 0], dst_ref=x_in.at[offset, j],
            send_sem=f_send.at[offset, j], recv_sem=f_recv.at[offset, j],
            device_id={"head": lax.rem(head + j, heads)}, device_id_type=MESH,
        )

    def page_copy(offset):
        return pltpu.make_async_remote_copy(
            src_ref=page_out.at[offset], dst_ref=pages.at[offset],
            send_sem=g_send.at[offset], recv_sem=g_recv.at[offset],
            device_id={"pool": frm(offset)}, device_id_type=MESH,
        )

    def line_copy(bufs, t, going_right):
        out, scale, inbound, scale_in, send, recv = bufs
        side = 0 if going_right else 1
        peer = me + 1 if going_right else me - 1
        return [
            pltpu.make_async_remote_copy(
                src_ref=source.at[t], dst_ref=target.at[side, t],
                send_sem=send.at[k, t], recv_sem=recv.at[side, k, t],
                device_id={"pool": peer}, device_id_type=MESH,
            )
            for k, (source, target) in enumerate(((scale, scale_in), (out, inbound)))
        ]

    def fresh_copy(offset):
        return pltpu.make_async_remote_copy(
            src_ref=fresh, dst_ref=fresh_all.at[offset],
            send_sem=r_send.at[offset], recv_sem=r_recv.at[offset],
            device_id={"pool": to(offset)}, device_id_type=MESH,
        )

    def far_first(send, toward):
        @pl.loop(0, pool - 1)
        def _(step):
            distance = pool - 1 - step

            @pl.when(me + distance < pool)
            def _():
                send(distance if toward else pool - distance)

            @pl.when(me - distance >= 0)
            def _():
                send(pool - distance if toward else distance)

    def send_hidden(offset):
        meta_copy(offset).start()
        x_copy(offset).start()

    far_first(send_hidden, True)

    own_meta = pltpu.make_async_copy(meta.at[me], meta_all.at[0], own_sem.at[0])
    own_meta.start()
    loads[0].wait()
    for c in range(capacity):
        page_out[0, c] = store[own_pick[me, c]]
    own_pages = pltpu.make_async_copy(page_out.at[0], pages.at[0], own_sem.at[1])
    own_pages.start()

    def pick_copy(offset):
        return pltpu.make_async_copy(
            meta_all.at[offset, :, pl.ds(0, 128)], picks.at[offset], pick_sem.at[offset]
        )

    @pl.loop(1, pool)
    def _(offset):
        meta_copy(offset).wait_recv()
        pick_copy(offset).start()
        pick_copy(offset).wait()
        for c in range(capacity):
            page_out[offset, c] = store[picks[offset, 0, c]]
        page_copy(offset).start()

    for load in loads[1:]:
        load.wait()
    tile = math.gcd(512, math.gcd(q_cols, kv_cols))

    def project(target, x_of, weight, base):
        @pl.loop(0, weight.shape[1] // tile)
        def _(n):
            cols = pl.ds(pl.multiple_of(n * tile, tile), tile)
            total = None
            for x, start in x_of:
                term = jnp.dot(
                    x[...], weight[pl.ds(start, x.shape[1]), cols],
                    preferred_element_type=jnp.float32,
                )
                total = term if total is None else total + term
            target[:, pl.ds(pl.multiple_of(base + n * tile, tile), tile)] = total

    project(own_acc, [(own_x, 0)], wkv, q_cols)
    project(own_acc, [(own_x, 0)], wq, 0)

    if share > 1:
        def pass_on(offset):
            x_copy(offset).wait_recv()
            for j in range(1, share):
                share_copy(offset, j).start()

        far_first(pass_on, False)

    def encode(bufs, t, base, blocks):
        values = acc[:, base:base + blocks * 128]
        peak = jnp.max(jnp.abs(values), axis=1, keepdims=True)
        scale = jnp.broadcast_to(jnp.maximum(peak * 1.005, 1e-30), (rows, 128)).astype(jnp.bfloat16)
        bufs[1][t] = scale
        inverse = LEVELS / scale.astype(jnp.float32)
        for quad in range(0, blocks, 4):
            packed = jnp.full((rows, 128), -32768, jnp.int32)
            for n in range(quad, min(quad + 4, blocks)):
                code = jnp.round(acc[:, base + n * 128:base + (n + 1) * 128] * inverse).astype(jnp.int32)
                bufs[0][t, :, n * 128:(n + 1) * 128] = (code >> 4).astype(jnp.int16)
                packed = packed + ((code & 15) << (4 * (n - quad)))
            lane = (blocks + quad // 4) * 128
            bufs[0][t, :, lane:lane + 128] = packed.astype(jnp.int16)

    def add_in(target, bufs, t, side, base, blocks):
        for copy in line_copy(bufs, t, side == 0):
            copy.wait_recv()
        factor = bufs[3][side, t].astype(jnp.float32) * (1.0 / LEVELS)
        for quad in range(0, blocks, 4):
            lane = (blocks + quad // 4) * 128
            packed = bufs[2][side, t, :, lane:lane + 128].astype(jnp.int32) + 32768
            for n in range(quad, min(quad + 4, blocks)):
                high = bufs[2][side, t, :, n * 128:(n + 1) * 128].astype(jnp.int32)
                code = high * 16 + ((packed >> (4 * (n - quad))) & 15)
                target[:, base + n * 128:base + (n + 1) * 128] += code.astype(jnp.float32) * factor

    def reduce_line(bufs, weight, base, first):
        blocks = weight.shape[1] // 128

        def serve(t, going_right):
            slot = lax.rem(me - t + pool, pool)
            pieces = []
            for j in range(share):
                if first:
                    if j:
                        share_copy(slot, j).wait_recv()
                    elif share == 1:
                        x_copy(slot).wait_recv()
                start = pl.multiple_of(lax.rem(head + heads - j, heads) * piece, piece) if share > 1 else 0
                pieces.append((x_in.at[slot, j], start))
            project(acc, pieces, weight, base)
            side = 0 if going_right else 1

            @pl.when(me > 0 if going_right else me < pool - 1)
            def _():
                add_in(acc, bufs, t, side, base, blocks)

            encode(bufs, t, base, blocks)
            for copy in line_copy(bufs, t, going_right):
                copy.start()

        @pl.loop(0, pool - 1)
        def _(step):
            distance = pool - 1 - step

            @pl.when(me + distance < pool)
            def _():
                serve(me + distance, True)

            @pl.when(me - distance >= 0)
            def _():
                serve(me - distance, False)

        @pl.when(me > 0)
        def _():
            add_in(own_acc, bufs, me, 0, base, blocks)

        @pl.when(me < pool - 1)
        def _():
            add_in(own_acc, bufs, me, 1, base, blocks)

    def finish_line(bufs):
        @pl.loop(0, pool)
        def _(t):
            @pl.when(t > me)
            def _():
                for copy in line_copy(bufs, t, True):
                    copy.wait_send()

            @pl.when(t < me)
            def _():
                for copy in line_copy(bufs, t, False):
                    copy.wait_send()

    kv_bufs = (kv_out, kv_scale, kv_in, kv_scale_in, kv_send, kv_recv)
    q_bufs = (q_part, q_scale, q_in, q_scale_in, q_send, q_recv)
    reduce_line(kv_bufs, wkv, q_cols, True)

    def rotated(cols):
        value = own_acc[:, cols]
        return (value * cosine[...] + pltpu.roll(value, HD // 2, 1) * sine[...]).astype(jnp.bfloat16)

    for n in range(kv_cols // HD):
        cols = slice(q_cols + n * HD, q_cols + (n + 1) * HD)
        block = rotated(cols) if n % 2 == 0 else own_acc[:, cols].astype(jnp.bfloat16)
        fresh[:, n * HD:(n + 1) * HD] = block

    @pl.loop(1, pool)
    def _(offset):
        fresh_copy(offset).start()

    own_fresh = pltpu.make_async_copy(fresh, fresh_all.at[0], own_sem.at[2])
    own_fresh.start()
    reduce_line(q_bufs, wq, 0, False)
    for n in range(q_cols // HD):
        q_out[:, n * HD:(n + 1) * HD] = rotated(slice(n * HD, (n + 1) * HD))

    own_meta.wait()
    own_pages.wait()
    own_fresh.wait()

    @pl.loop(1, pool)
    def _(offset):
        fresh_copy(offset).wait_recv()
        page_copy(offset).wait_recv()
        meta_copy(offset).wait_send()
        x_copy(offset).wait_send()
        for j in range(1, share):
            share_copy(offset, j).wait_send()
        page_copy(offset).wait_send()
        fresh_copy(offset).wait_send()

    finish_line(kv_bufs)
    finish_line(q_bufs)


def attend_kernel(
    pool,
    gather, q, fresh_all, pages, goals, store, pos_row,
    attended, new_store,
    context,
):
    sessions, context_pages = gather.shape
    page_len, width = store.shape[1:]
    context_len = context_pages * page_len
    rows, q_cols = q.shape
    pick = rows // sessions
    local_kv = width // (2 * HD)
    group = q_cols // HD // local_kv
    for s in range(sessions):
        @pl.loop(0, context_pages)
        def _(p):
            context[pl.ds(pl.multiple_of(p * page_len, page_len), page_len), :] = pages[gather[s, p]]

        token = lax.broadcasted_iota(jnp.int32, (context_len, pick), 0)
        hot = jnp.where(token == pos_row[s], 1.0, 0.0).astype(jnp.bfloat16)
        taken = jnp.dot(hot, jnp.ones((pick, HD), jnp.bfloat16), preferred_element_type=jnp.float32) > 0.5
        mine = fresh_all[s * pick:(s + 1) * pick, :]
        for n in range(width // HD):
            cols = slice(n * HD, (n + 1) * HD)
            spread = jnp.dot(hot, mine[:, cols], preferred_element_type=jnp.float32)
            context[:, cols] = jnp.where(
                taken, spread, context[:, cols].astype(jnp.float32)
            ).astype(jnp.bfloat16)
        diagonal = lax.broadcasted_iota(jnp.int32, (pick, pick), 0) == lax.broadcasted_iota(
            jnp.int32, (pick, pick), 1
        )
        spot = jnp.sum(
            jnp.where(diagonal, pos_row[s].astype(jnp.float32), 0.0), axis=1, keepdims=True
        ).astype(jnp.int32)
        limit = jnp.concatenate([spot] * group, axis=0)
        column = lax.broadcasted_iota(jnp.int32, (group * pick, context_len), 1)
        allowed = column <= limit
        for k in range(local_kv):
            keys = context[:, 2 * k * HD:(2 * k + 1) * HD]
            vals = context[:, (2 * k + 1) * HD:(2 * k + 2) * HD]
            heads = jnp.concatenate(
                [
                    q[s * pick:(s + 1) * pick, (k * group + g) * HD:(k * group + g + 1) * HD]
                    for g in range(group)
                ],
                axis=0,
            )
            scores = lax.dot_general(
                heads, keys, (((1,), (1,)), ((), ())), preferred_element_type=jnp.float32
            ) * (1.0 / math.sqrt(HD))
            scores = jnp.where(allowed, scores, -jnp.inf)
            exps = jnp.exp(scores - jnp.max(scores, axis=1, keepdims=True))
            weights = (exps * (1.0 / jnp.sum(exps, axis=1, keepdims=True))).astype(jnp.bfloat16)
            out = jnp.dot(weights, vals, preferred_element_type=jnp.float32).astype(jnp.bfloat16)
            for g in range(group):
                attended[s * pick:(s + 1) * pick, (k * group + g) * HD:(k * group + g + 1) * HD] = (
                    out[g * pick:(g + 1) * pick]
                )

    held = store.shape[0]
    chunk = next(c for c in (8, 6, 4, 3, 2, 1) if held % c == 0)
    span = chunk * page_len

    @pl.loop(0, held // chunk)
    def _(b):
        slots = pl.ds(b * chunk, chunk)
        first = lax.axis_index("pool") * held * page_len + b * span
        place = first + lax.broadcasted_iota(jnp.int32, (span, pool * rows), 0)
        hot = jnp.where(place == goals[...], 1.0, 0.0).astype(jnp.bfloat16)
        count = jnp.dot(
            hot, jnp.ones((pool * rows, HD), jnp.bfloat16), preferred_element_type=jnp.float32
        )
        taken = count > 0.5
        for n in range(width // HD):
            cols = slice(n * HD, (n + 1) * HD)
            old = store[slots, :, cols].reshape(span, HD).astype(jnp.float32)
            total = jnp.dot(hot, fresh_all[:, cols], preferred_element_type=jnp.float32)
            new = jnp.where(taken, total, old).astype(jnp.bfloat16)
            new_store[slots, :, cols] = new.reshape(chunk, page_len, HD)


def body(hidden, select, page_table, kv_store, w_query, w_kv):
    rows = hidden.shape[0]
    sessions, pick_count = select.shape
    held_slots, page_len, width = kv_store.shape
    depth, q_cols = w_query.shape
    kv_cols = w_kv.shape[1]
    pool = lax.axis_size("pool")
    heads = lax.axis_size("head")
    me = lax.axis_index("pool")
    share = heads if depth % (128 * heads) == 0 else 1
    context_pages = page_table.shape[1]
    entry_count = sessions * context_pages
    capacity = max(2, 2 * ((entry_count + 2 * pool - 1) // (2 * pool)))
    lanes = 128 * ((max(rows, capacity) + 127) // 128)

    positions = select.reshape(rows)
    half = HD // 2
    freqs = jnp.power(jnp.float32(ROPE_BASE), -(jnp.arange(half, dtype=jnp.float32) * 2.0 / HD))
    angles = positions.astype(jnp.float32)[:, None] * freqs[None, :]
    cosine = jnp.cos(angles)
    sine = jnp.sin(angles)
    cosine = jnp.concatenate([cosine, cosine], axis=1)
    sine = jnp.concatenate([-sine, sine], axis=1)

    table = page_table.reshape(entry_count)
    is_live, holder_of, rank_of = holder_rank(table, held_slots)
    target = jnp.where(is_live, holder_of * capacity + rank_of, -1)
    own_slots = table % held_slots
    request = jnp.max(
        jnp.where(target[:, None] == jnp.arange(pool * capacity)[None, :], own_slots[:, None], 0),
        axis=0,
    ).reshape(pool, capacity).astype(jnp.int32)
    page_of = select // page_len
    slot_of = jnp.max(
        jnp.where(page_of[:, :, None] == jnp.arange(context_pages)[None, None], page_table[:, None, :], -1),
        axis=2,
    )
    goal = (slot_of * page_len + select % page_len).reshape(1, rows)
    meta = jnp.concatenate(
        [
            jnp.pad(request, ((0, 0), (0, lanes - capacity)))[:, None, :],
            jnp.broadcast_to(jnp.pad(goal, ((0, 0), (0, lanes - rows)))[None], (pool, 1, lanes)),
            jnp.zeros((pool, 6, lanes), jnp.int32),
        ],
        axis=1,
    ).astype(jnp.int32)
    relative = jnp.where(is_live, (holder_of - me + pool) % pool, 0)
    gather = jnp.where(is_live, relative * capacity + rank_of, 0).reshape(sessions, context_pages)
    gather = gather.astype(jnp.int32)

    bf16, f32, i32 = jnp.bfloat16, jnp.float32, jnp.int32
    cols = q_cols + kv_cols
    dma = pltpu.SemaphoreType.DMA

    def line_scratch(width):
        coded = width + 128 * ((width // 128 + 3) // 4)
        return (
            pltpu.VMEM((pool, rows, coded), jnp.int16),
            pltpu.VMEM((pool, rows, 128), bf16),
            pltpu.VMEM((2, pool, rows, coded), jnp.int16),
            pltpu.VMEM((2, pool, rows, 128), bf16),
        )

    q, fresh_all, pages, meta_all = pl.pallas_call(
        functools.partial(exchange_kernel, pool, heads, share, capacity),
        out_shape=(
            jax.ShapeDtypeStruct((rows, q_cols), bf16),
            jax.ShapeDtypeStruct((pool, rows, kv_cols), bf16),
            jax.ShapeDtypeStruct((pool, capacity, page_len, width), bf16),
            jax.ShapeDtypeStruct((pool, 8, lanes), i32),
        ),
        in_specs=[ANY, ANY, ANY, ANY, ANY, SMEM, VMEM, VMEM],
        out_specs=(VMEM, ANY, ANY, ANY),
        scratch_shapes=[
            pltpu.VMEM((depth, q_cols), bf16),
            pltpu.VMEM((depth, kv_cols), bf16),
            pltpu.VMEM((held_slots, page_len, width), bf16),
            pltpu.VMEM((rows, depth), bf16),
            pltpu.VMEM((pool, share, rows, depth // share), bf16),
            pltpu.VMEM((rows, cols), f32),
            pltpu.VMEM((rows, cols), f32),
            *line_scratch(kv_cols),
            *line_scratch(q_cols),
            pltpu.VMEM((pool, capacity, page_len, width), bf16),
            pltpu.VMEM((rows, kv_cols), bf16),
            pltpu.SMEM((pool, 8, 128), i32),
            dma((4,)),
            dma((pool,)), dma((pool,)),
            dma((pool, share)), dma((pool, share)),
            dma((pool,)), dma((pool,)), dma((pool,)),
            dma((pool,)), dma((pool,)),
            dma((2, pool)), dma((2, 2, pool)),
            dma((2, pool)), dma((2, 2, pool)),
            dma((pool,)), dma((pool,)),
            dma((3,)),
        ],
        compiler_params=pltpu.CompilerParams(
            collective_id=0, has_side_effects=True, vmem_limit_bytes=VMEM_BYTES
        ),
    )(meta, hidden, w_query, w_kv, kv_store, request, cosine, sine)

    goals = meta_all[:, 1, :rows].reshape(1, pool * rows)
    attended, new_store = pl.pallas_call(
        functools.partial(attend_kernel, pool),
        out_shape=(
            jax.ShapeDtypeStruct((rows, q_cols), bf16),
            jax.ShapeDtypeStruct(kv_store.shape, bf16),
        ),
        in_specs=[SMEM] + [VMEM] * 6,
        out_specs=(VMEM, VMEM),
        scratch_shapes=[pltpu.VMEM((context_pages * page_len, width), bf16)],
        compiler_params=pltpu.CompilerParams(vmem_limit_bytes=VMEM_BYTES),
    )(
        gather, q, fresh_all.reshape(pool * rows, kv_cols),
        pages.reshape(pool * capacity, page_len, width), goals, kv_store,
        select.reshape(sessions, 1, pick_count),
    )
    return attended, new_store


def solution(mesh):
    return jax.shard_map(
        body,
        mesh=mesh,
        in_specs=(
            P(("groups", "pool"), None),
            P(("groups", "pool"), None),
            P(("groups", "pool"), None),
            P(("groups", "pool"), None, "head"),
            P("pool", "head"),
            P("pool", "head"),
        ),
        out_specs=(P(("groups", "pool"), "head"), P(("groups", "pool"), None, "head")),
        check_vma=False,
    )
```
